128 devices in a mesh: cache: 32 (over x, y, core), tp: 4 (over z).
Axes of the slice: x: 4, y: 4, z: 4, core: 2. Of those that a mesh axis runs over, the one named last changes fastest.
Arguments:
- queries: bfloat16 [65536, 2048], P('cache', 'tp'), may hold values from -6 to 6
- key_vecs: bfloat16 [65536, 2048], P('cache', 'tp'), may hold values from -6 to 6
- values: bfloat16 [65536, 2048], P('cache', 'tp'), may hold values from -6 to 6
- log_decay: bfloat16 [65536, 2048], P('cache', 'tp'), may hold values from -2 to 0
- write_strength: float32 [65536, 16], P('cache', 'tp'), may hold values from 0.2 to 0.9
- inverses: float32 [1024, 64, 1024], P('cache', None, 'tp'), may hold values from -1 to 1
- suffix_stretches: int32 [512], P('cache'), may hold values from 1 to 2, 768 in all
- ckpt_store: float32 [64, 16, 128, 128], P('cache', 'tp'), may hold values from -4 to 4
- hit_owner: int32 [512], P('cache'), may hold values from 0 to 31, as said below
- hit_slot: int32 [512], P('cache'), may hold values from 0 to 1
- ret_owner: int32 [512], P('cache'), may hold values from 0 to 31, as said below
- out_gate: bfloat16 [65536, 2048], P('cache', 'tp'), may hold values from -6 to 6
- norm_gain: float32 [128], replicated, may hold values from 0.1 to 1.9
- out_weight: bfloat16 [2048, 2304], P('tp'), may hold values from -0.125 to 0.125
Outputs:
- mixed: bfloat16 [65536, 2304], P(('cache', 'tp'))
- new_ckpts: float32 [512, 16, 128, 128], P('cache', 'tp')
The draws below stay inside these ranges and needn't reach their ends.
Inputs may be any that keep to these rules, and one draw needn't show every extreme that they name: `hit_owner`: within each index of cache's block of 16 requests, no owner is named more than 1 times, and in every block some owner is named exactly 1 times; for each position r within the blocks, every owner is named at position r by exactly one block. `ret_owner`: within each index of cache's block of 16 requests, no owner is named more than 1 times, and in every block some owner is named exactly 1 times; for each position r within the blocks, every owner is named at position r by exactly one block.
All inputs are finite; a program needn't handle non-finite values. No bound on the sum of `suffix_stretches` on one device may be relied on, other than what follows from the above.
Results may differ from the reference program's by a relative error of at most 0.018.
Values may be sent and summed in bfloat16 or wider, within the bound.
No kernel may reach another device: no remote copies, remote signals or barrier semaphores. Data moves between devices by JAX's collectives and lax.ppermute only.
A program may use at most 192 MiB of HBM per device.

```python
import math
import jax
import jax.numpy as jnp
import numpy as np
from jax import lax

D = 2304
SHARD_ATTN_COUNT = 16
DK = 128
DV = 128
CH = 64
MAXCH = 2
R_DEV = 16
CK_DEV = 2
QUERY_JOB_COUNT = 512
TOKENS = 65536
CKPTS = 64
N_TP = 4


def owner_table(key):
    devices = QUERY_JOB_COUNT // R_DEV
    capacity = (R_DEV + devices - 1) // devices
    key_place, key_label, key_offset = jax.random.split(key, 3)
    placing = jax.random.permutation(key_place, devices)
    relabel = jax.random.permutation(key_label, devices)
    offsets = jax.random.permutation(key_offset, devices * capacity)[:R_DEV] % devices
    table = relabel[(placing[:, None] + offsets[None, :]) % devices]
    return table.reshape(QUERY_JOB_COUNT).astype(jnp.int32)


def draw_hit_owner(key, part):
    key = jax.random.fold_in(key, 11)
    return owner_table(key)


def draw_ret_owner(key, part):
    key = jax.random.fold_in(key, 23)
    return owner_table(key)


def draw_log_decay(key, part):
    key = jax.random.fold_in(key, 37)
    speed_rng_key, job_rng_key, jagged_rng_key, spurt_rng_key, backlog_rng_key = jax.random.split(key, 5)
    low_rate, high_rate = (0.001, 0.03)
    piece_entries = MAXCH * CH
    fading_speed = jnp.exp(jax.random.uniform(speed_rng_key, (1, 1, SHARD_ATTN_COUNT, DK), jnp.float32, math.log(low_rate), math.log(high_rate)))
    job_word_counts = jax.random.uniform(job_rng_key, (QUERY_JOB_COUNT, 1, SHARD_ATTN_COUNT, DK), jnp.float32, 0.5, 2.0)
    jaggedness = jax.random.uniform(jagged_rng_key, (QUERY_JOB_COUNT, piece_entries, SHARD_ATTN_COUNT, DK), jnp.float32, 0.5, 1.5)
    spurt_spans = jax.random.bernoulli(spurt_rng_key, 1.0 / 40.0, (QUERY_JOB_COUNT, piece_entries, SHARD_ATTN_COUNT, 1))
    backlog_span = jax.random.uniform(backlog_rng_key, (QUERY_JOB_COUNT, piece_entries, SHARD_ATTN_COUNT, 1), jnp.float32, math.log(0.5), math.log(0.8))
    fading_multipliers = -fading_speed * job_word_counts * jaggedness + jnp.where(spurt_spans, backlog_span, 0.0)
    return fading_multipliers.reshape(TOKENS, SHARD_ATTN_COUNT * DK).astype(jnp.bfloat16)


def draw_inverses(key, part):
    key = jax.random.fold_in(key, 41)
    shape_all = (QUERY_JOB_COUNT * MAXCH, CH, SHARD_ATTN_COUNT, CH)
    off_diag = 0.1 * jax.random.normal(key, shape_all, jnp.float32)
    positions = jnp.arange(CH)
    below = (positions[:, None] > positions[None, :])[None, :, None, :]
    on_diag = (positions[:, None] == positions[None, :])[None, :, None, :]
    matrices = jnp.where(below, jnp.clip(off_diag, -0.9, 0.9), 0.0) + jnp.where(on_diag, 1.0, 0.0)
    return matrices.reshape(QUERY_JOB_COUNT * MAXCH, CH, SHARD_ATTN_COUNT * CH).astype(jnp.float32)


def set_ends(drawn, key, least, top_value):
    longest = drawn.shape.index(max(drawn.shape))
    spots = []
    for shift in (0, 1):
        where = [jax.random.randint(jax.random.fold_in(key, axis), (), 0, length) for axis, length in enumerate(drawn.shape)]
        where[longest] = (where[longest] + shift) % drawn.shape[longest]
        spots.append(tuple(where))
    return drawn.at[spots[0]].set(least).at[spots[1]].set(top_value)


def level_of(stream_key, dims, cuts, low, high):
    factor_of, own = 1.0, jax.random.fold_in(stream_key, 6)
    for dim, parts in cuts:
        heights = jnp.exp(jax.random.uniform(jax.random.fold_in(own, dim), (parts,), jnp.float32, low / len(cuts), high / len(cuts)))
        factor_of = factor_of * jnp.repeat(heights, dims[dim] // parts).reshape([-1 if axis == dim else 1 for axis in range(len(dims))])
    return factor_of


def split_up(amount, total, reach, lean):
    weights = [(1 << 20) // math.isqrt(standing ** lean) + 1 for standing in range(2, amount + 1)]
    spare, given = total - reach - (amount - 1), [1] * (amount - 1)
    while spare > 0:
        free = [i for i in range(amount - 1) if given[i] < reach]
        pool, remaining = sum([weights[i] for i in free]), spare
        for i in free:
            more = min(reach - given[i], max(1, remaining * weights[i] // pool), spare)
            given[i] = given[i] + more
            spare = spare - more
    return np.array([reach] + given)


def uneven_parts(stream_key, number_of, total, bound, slope):
    if number_of == 2:
        one = jax.random.randint(stream_key, (), max(1, total - bound), min(bound, total - 1) + 1)
        return jnp.stack([one, total - one])
    sizes = jnp.asarray(split_up(number_of, total, bound, slope), jnp.int32)
    pairs = (number_of - 1) // 2
    donor, receiver = sizes[1:1 + 2 * pairs:2], sizes[2:2 + 2 * pairs:2]
    margin = jnp.minimum(donor - 1, bound - receiver)
    passed = jax.random.randint(jax.random.fold_in(stream_key, 1), (pairs,), 0, 1 << 20) % (margin + 1)
    sizes = sizes.at[1:1 + 2 * pairs:2].set(donor - passed).at[2:2 + 2 * pairs:2].set(receiver + passed)
    return sizes[jax.random.permutation(jax.random.fold_in(stream_key, 2), number_of)]


def noise(rng, shape, width, most, cuts=(), kind=jnp.bfloat16):
    entries = jax.random.normal(rng, shape, jnp.float32) * width
    if len(cuts) > 0:
        entries = level_of(rng, shape, cuts, -0.22, 0.18) * entries
    return jnp.clip(entries, min=-most, max=most).astype(kind)


def setup_inputs(seed: int = 0) -> dict:
    key_of = jax.random.split(jax.random.key(seed), 15)
    return {
        "queries": noise(key_of[0], (TOKENS, SHARD_ATTN_COUNT * DK), 1.0, 6.0, ((0, 32), (1, 4))),
        "key_vecs": noise(key_of[1], (TOKENS, SHARD_ATTN_COUNT * DK), 1.0, 6.0, ((0, 32), (1, 4))),
        "values": noise(key_of[2], (TOKENS, SHARD_ATTN_COUNT * DV), 1.0, 6.0, ((0, 32), (1, 4))),
        "log_decay": draw_log_decay(jax.random.fold_in(key_of[14], 71), 0),
        "write_strength": jnp.clip(0.2 + 0.7 * jax.random.uniform(key_of[4], (TOKENS, SHARD_ATTN_COUNT), jnp.float32) ** level_of(key_of[4], (TOKENS, SHARD_ATTN_COUNT), ((0, 32), (1, 4)), -0.2, 0.2), 0.2, 0.9),
        "inverses": draw_inverses(jax.random.fold_in(key_of[14], 71), 0),
        "suffix_stretches": uneven_parts(key_of[6], QUERY_JOB_COUNT, QUERY_JOB_COUNT * (MAXCH + 1) // 2, MAXCH, 1).astype(jnp.int32),
        "ckpt_store": noise(key_of[7], (CKPTS, SHARD_ATTN_COUNT, DK, DV), 0.5, 4.0, ((0, 32), (1, 4)), jnp.float32),
        "hit_owner": draw_hit_owner(jax.random.fold_in(key_of[14], 71), 0),
        "hit_slot": set_ends(jax.random.randint(key_of[9], (QUERY_JOB_COUNT,), 0, CK_DEV), jax.random.fold_in(key_of[9], 1), 0, CK_DEV - 1).astype(jnp.int32),
        "ret_owner": draw_ret_owner(jax.random.fold_in(key_of[14], 71), 0),
        "out_gate": noise(key_of[11], (TOKENS, SHARD_ATTN_COUNT * DV), 1.0, 6.0, ((0, 32), (1, 4))),
        "norm_gain": jnp.clip(1.0 + 0.18 * jax.random.normal(key_of[12], (DV,), jnp.float32), 0.1, 1.9),
        "out_weight": noise(key_of[13], (SHARD_ATTN_COUNT * DV, D), (SHARD_ATTN_COUNT * DV) ** -0.5, 0.125, ((0, 4),)),
    }


HIGHEST_PRECISION = lax.Precision.HIGHEST

def unit_rows(matrix):
    return matrix / jnp.sqrt(lax.optimization_barrier(jnp.sum(matrix * matrix, axis=-1, keepdims=True)) + 1e-06)

def stretch_update(carry_state, q_stretch, k_stretch, v_stretch, g_stretch, b_stretch, m_stretch):
    cumulative = jnp.cumsum(g_stretch, axis=1)
    key_fwd = k_stretch * jnp.exp(cumulative)
    key_back = k_stretch * jnp.exp(-cumulative)
    query_fwd = q_stretch * jnp.exp(cumulative)
    key_end = k_stretch * jnp.exp(cumulative[:, -1:] - cumulative)
    w_matrix = jnp.einsum('rihj,rjhd->rihd', m_stretch, b_stretch[..., None] * key_fwd, precision=HIGHEST_PRECISION)
    u_matrix = jnp.einsum('rihj,rjhe->rihe', m_stretch, b_stretch[..., None] * v_stretch, precision=HIGHEST_PRECISION)
    new_values = u_matrix - jnp.einsum('rihd,rhde->rihe', w_matrix, carry_state, precision=HIGHEST_PRECISION)
    positions = jnp.arange(q_stretch.shape[1])
    lower_mask = positions[:, None] >= positions[None, :]
    intra_scores = jnp.einsum('rihd,rjhd->rhij', query_fwd, key_back, precision=HIGHEST_PRECISION)
    intra_scores = jnp.where(lower_mask, intra_scores, 0.0)
    result = jnp.einsum('rihd,rhde->rihe', query_fwd, carry_state, precision=HIGHEST_PRECISION)
    result = result + jnp.einsum('rhij,rjhe->rihe', intra_scores, new_values, precision=HIGHEST_PRECISION)
    next_state = jnp.exp(cumulative[:, -1])[..., None] * carry_state
    next_state = next_state + jnp.einsum('rjhd,rjhe->rhde', key_end, new_values, precision=HIGHEST_PRECISION)
    return (next_state, result)

def suffix_block(queries, key_vecs, values, log_decay, write_strength, inverses, counts, carry_state, gates, gain_vec):
    head_count = write_strength.shape[-1]
    request_count = counts.shape[0]
    piece_entries = queries.shape[0] // request_count
    stretch_count = piece_entries // CH
    shape_k = (request_count, stretch_count, CH, head_count, DK)
    shape_v = (request_count, stretch_count, CH, head_count, DV)
    q_unit = unit_rows(queries.astype(jnp.float32).reshape(shape_k))
    k_unit = unit_rows(key_vecs.astype(jnp.float32).reshape(shape_k))
    v_rows = values.astype(jnp.float32).reshape(shape_v)
    fading_multipliers = log_decay.astype(jnp.float32).reshape(shape_k)
    strengths = write_strength.reshape(request_count, stretch_count, CH, head_count)
    matrices = inverses.reshape(request_count, stretch_count, CH, head_count, CH)
    outputs = []
    for stretch_index in range(stretch_count):
        next_state, result = stretch_update(carry_state, q_unit[:, stretch_index], k_unit[:, stretch_index], v_rows[:, stretch_index], fading_multipliers[:, stretch_index], strengths[:, stretch_index], matrices[:, stretch_index])
        live_mask = (stretch_index < counts)[:, None, None, None]
        carry_state = jnp.where(live_mask, next_state, carry_state)
        outputs.append(jnp.where(live_mask, result, 0.0))
    head_out = jnp.stack(outputs, axis=1).reshape(request_count * piece_entries, head_count, DV)
    mean_square = lax.optimization_barrier(jnp.mean(head_out * head_out, axis=-1, keepdims=True))
    normed = head_out / jnp.sqrt(mean_square + 1e-05) * gain_vec
    gated_out = normed.reshape(request_count * piece_entries, head_count * DV) * jax.nn.sigmoid(gates.astype(jnp.float32))
    return (carry_state, gated_out.astype(jnp.bfloat16))

def reference(queries, key_vecs, values, log_decay, write_strength, inverses, suffix_stretches, ckpt_store, hit_owner, hit_slot, ret_owner, out_gate, norm_gain, out_weight):
    blocks = QUERY_JOB_COUNT // R_DEV
    row_count = R_DEV * MAXCH * CH
    initial = ckpt_store[(hit_owner * CK_DEV + hit_slot).astype(jnp.int32)]
    weight_wide = out_weight.astype(jnp.float32)
    group_width = SHARD_ATTN_COUNT * DV // N_TP

    def one_block(block_item):
        q_blk, k_blk, v_blk, g_blk, b_blk, m_blk, c_blk, s_blk, t_blk = block_item
        final_states, gated_out = suffix_block(q_blk, k_blk, v_blk, g_blk, b_blk, m_blk, c_blk, s_blk, t_blk, norm_gain)
        accum = jnp.zeros((row_count, D), jnp.float32)
        for tp_group in range(N_TP):
            lo_col = tp_group * group_width
            partial_value = jnp.dot(gated_out[:, lo_col:lo_col + group_width].astype(jnp.float32), weight_wide[lo_col:lo_col + group_width], preferred_element_type=jnp.float32)
            accum = accum + lax.optimization_barrier(partial_value.astype(jnp.bfloat16)).astype(jnp.float32)
        return (final_states, accum.astype(jnp.bfloat16))
    finals, mixed = lax.map(one_block, (queries.reshape(blocks, row_count, SHARD_ATTN_COUNT * DK), key_vecs.reshape(blocks, row_count, SHARD_ATTN_COUNT * DK), values.reshape(blocks, row_count, SHARD_ATTN_COUNT * DV), log_decay.reshape(blocks, row_count, SHARD_ATTN_COUNT * DK), write_strength.reshape(blocks, row_count, SHARD_ATTN_COUNT), inverses.reshape(blocks, R_DEV * MAXCH, CH, SHARD_ATTN_COUNT * CH), suffix_stretches.reshape(blocks, R_DEV), initial.reshape(blocks, R_DEV, SHARD_ATTN_COUNT, DK, DV), out_gate.reshape(blocks, row_count, SHARD_ATTN_COUNT * DV)))
    finals = finals.reshape(QUERY_JOB_COUNT, SHARD_ATTN_COUNT, DK, DV)
    target = (ret_owner * R_DEV + jnp.arange(QUERY_JOB_COUNT, dtype=jnp.int32) % R_DEV).astype(jnp.int32)
    new_ckpts = jnp.zeros((QUERY_JOB_COUNT, SHARD_ATTN_COUNT, DK, DV), jnp.float32).at[target].set(finals)
    return (mixed.reshape(TOKENS, D), new_ckpts)
```

```python
import jax
import jax.numpy as jnp
from jax import lax
from jax.experimental import pallas as pl
from jax.experimental.pallas import tpu as pltpu
from jax.sharding import PartitionSpec as P

DK = 128
DV = 128
CH = 64
MAXCH = 2
R_DEV = 16
HEADS = 4
PAIRS = HEADS // 2
CACHE = 32
N_TP = 4
D = 2304
HALF = D // 2
WIDTH = HEADS * DK
ROWS = MAXCH * CH
TAG_ROWS = 16
QUARTER_SHIFTS = (2, 1, 3, 0)

f32 = jnp.float32
bf16 = jnp.bfloat16


def block_diagonal(left, right):
    zeros = jnp.zeros_like(left)
    return jnp.concatenate(
        [jnp.concatenate([left, zeros], axis=1), jnp.concatenate([zeros, right], axis=1)],
        axis=0,
    )


def pair_diagonal(pair):
    return block_diagonal(pair[:, :DK], pair[:, DK:])


def side_by_side(left, right):
    return jnp.concatenate([left, right], axis=1)


def prepare_kernel(
    counts_ref, q_ref, k_ref, v_ref, g_ref, b_ref, m_ref, wq_ref, u_ref, lk_ref, d_ref
):
    lower = lax.broadcasted_iota(jnp.int32, (CH, CH), 0) >= lax.broadcasted_iota(
        jnp.int32, (CH, CH), 1
    )
    summing = jnp.where(lower, 1.0, 0.0).astype(bf16)
    row = lax.broadcasted_iota(jnp.int32, (CH, 2 * CH), 0)
    column = lax.broadcasted_iota(jnp.int32, (CH, 2 * CH), 1)
    causal = row >= lax.rem(column, CH)
    decays = []
    for c in range(MAXCH):
        rows = pl.ds(c * CH, CH)
        cumulative = jnp.dot(summing, g_ref[rows, :], preferred_element_type=f32)
        for p in range(PAIRS):
            query_fwd, key_fwd, key_back, key_end, strong_values = [], [], [], [], []
            for h in (2 * p, 2 * p + 1):
                lanes = pl.ds(h * DK, DK)
                q = q_ref[rows, lanes].astype(f32)
                k = k_ref[rows, lanes].astype(f32)
                v = v_ref[rows, lanes].astype(f32)
                strength = b_ref[rows, h : h + 1]
                cum = cumulative[:, h * DK : (h + 1) * DK]
                last = cum[CH - 1 : CH, :]
                forward = jnp.exp(cum)
                q_unit = q * lax.rsqrt(jnp.sum(q * q, axis=1, keepdims=True) + 1e-06)
                k_unit = k * lax.rsqrt(jnp.sum(k * k, axis=1, keepdims=True) + 1e-06)
                query_fwd.append((q_unit * forward).astype(bf16))
                key_fwd.append((strength * (k_unit * forward)).astype(bf16))
                key_back.append((k_unit * jnp.exp(-cum)).astype(bf16))
                key_end.append(k_unit * jnp.exp(last - cum))
                strong_values.append((strength * v).astype(bf16))
                decays.append(jnp.exp(last))
            wide = pl.ds(p * 2 * DK, 2 * DK)
            narrow = pl.ds(p * 2 * CH, 2 * CH)
            inverse = m_ref[c, :, narrow].astype(bf16)
            w = jnp.dot(inverse, block_diagonal(*key_fwd), preferred_element_type=f32)
            u = jnp.dot(inverse, block_diagonal(*strong_values), preferred_element_type=f32)
            queries = side_by_side(*query_fwd)
            scores = lax.dot_general(
                queries,
                block_diagonal(*key_back),
                (((1,), (1,)), ((), ())),
                preferred_element_type=f32,
            )
            wq_ref[0, c, pl.ds(0, CH), wide] = w.astype(bf16)
            wq_ref[0, c, pl.ds(CH, CH), wide] = queries
            u_ref[0, c, :, wide] = u.astype(bf16)
            lk_ref[0, c, pl.ds(0, CH), narrow] = jnp.where(causal, scores, 0.0).astype(bf16)
            lk_ref[0, c, pl.ds(CH, DK), narrow] = jnp.concatenate(key_end, axis=0).T.astype(bf16)
    d_ref[0] = jnp.concatenate(decays, axis=0).T


def advance_kernel(
    order_ref,
    hit_ref,
    ret_ref,
    counts_ref,
    s_ref,
    wq_ref,
    u_ref,
    lk_ref,
    d_ref,
    gate_ref,
    gain_ref,
    far_ref,
    next_ref,
    back_ref,
    own_ref,
    send_ref,
    gated_ref,
):
    step = pl.program_id(0)
    live = counts_ref[order_ref[step]] > 1
    gain = gain_ref[...]

    def put_gated(c, p, out):
        for side in range(2):
            h = 2 * p + side
            rows, lanes = pl.ds(c * CH, CH), pl.ds(h * DV, DV)
            head_out = out[:, side * DV : (side + 1) * DV]
            mean_square = jnp.mean(head_out * head_out, axis=1, keepdims=True)
            normed = head_out * lax.rsqrt(mean_square + 1e-05) * gain
            gate = gate_ref[rows, lanes].astype(f32)
            gated_ref[rows, lanes] = (normed * jax.nn.sigmoid(gate)).astype(bf16)

    def stretch(c, p, state_pair, diagonal):
        wide = pl.ds(p * 2 * DK, 2 * DK)
        narrow = pl.ds(p * 2 * CH, 2 * CH)
        read = jnp.dot(wq_ref[0, c, :, wide], diagonal, preferred_element_type=f32)
        new_values = (u_ref[0, c, :, wide].astype(f32) - read[:CH]).astype(bf16)
        written = jnp.dot(
            lk_ref[0, c, :, narrow], pair_diagonal(new_values), preferred_element_type=f32
        )
        out = read[CH:] + written[:CH]
        states = []
        for side in range(2):
            at = c * HEADS + 2 * p + side
            decay = d_ref[0, :, at : at + 1]
            states.append(decay * state_pair[side] + written[CH:, side * DV : (side + 1) * DV])
        return out, states

    finals = []
    for p in range(PAIRS):
        left, right = s_ref[0, pl.ds(2 * p * DK, DK), :], s_ref[0, pl.ds((2 * p + 1) * DK, DK), :]
        out, states = stretch(
            0, p, (left.astype(f32), right.astype(f32)), block_diagonal(left, right)
        )
        put_gated(0, p, out)
        finals.append(states)

    @pl.when(live)
    def _():
        for p in range(PAIRS):
            states = finals[p]
            diagonal = block_diagonal(*[s.astype(bf16) for s in states])
            out, states = stretch(1, p, states, diagonal)
            put_gated(1, p, out)
            for side in range(2):
                send_ref[0, pl.ds((2 * p + side) * DK, DK), :] = states[side].astype(bf16)

    @pl.when(jnp.logical_not(live))
    def _():
        for p in range(PAIRS):
            for side in range(2):
                send_ref[0, pl.ds((2 * p + side) * DK, DK), :] = finals[p][side].astype(bf16)
        gated_ref[pl.ds(CH, CH), :] = jnp.zeros((CH, WIDTH), bf16)

    quarter = step // (R_DEV // N_TP)
    for index, out_ref in enumerate((far_ref, next_ref, back_ref, own_ref)):

        @pl.when(quarter == index)
        def _(out_ref=out_ref):
            out_ref[...] = gated_ref[...]


def project_kernel(core_ref, *refs):
    gated, own_ref, direct, swapped = refs[:4], refs[4], refs[5:8], refs[8:11]
    out_ref = refs[11]

    def total(others):
        acc = jnp.dot(gated[3][...], own_ref[...], preferred_element_type=f32)
        for rows_ref, weight_ref in zip(gated[:3], others):
            acc = acc + jnp.dot(rows_ref[...], weight_ref[...], preferred_element_type=f32)
        return acc.astype(bf16)

    @pl.when(pl.program_id(0) == 0)
    def _():
        out_ref[...] = total(direct)

    @pl.when(pl.program_id(0) == 1)
    def _():
        out_ref[...] = total(swapped)


def unpack_kernel(source_ref, in_ref, out_ref):
    out_ref[...] = in_ref[...].astype(f32)


def prepare(counts, queries, key_vecs, values, log_decay, write_strength, inverses):
    token_rows = pl.BlockSpec((ROWS, WIDTH), lambda i, n: (i, 0))
    return pl.pallas_call(
        prepare_kernel,
        grid_spec=pltpu.PrefetchScalarGridSpec(
            num_scalar_prefetch=1,
            grid=(R_DEV,),
            in_specs=[token_rows] * 4
            + [
                pl.BlockSpec((ROWS, HEADS), lambda i, n: (i, 0)),
                pl.BlockSpec((MAXCH, CH, HEADS * CH), lambda i, n: (i, 0, 0)),
            ],
            out_specs=[
                pl.BlockSpec((1, MAXCH, 2 * CH, WIDTH), lambda i, n: (i, 0, 0, 0)),
                pl.BlockSpec((1, MAXCH, CH, WIDTH), lambda i, n: (i, 0, 0, 0)),
                pl.BlockSpec((1, MAXCH, CH + DK, HEADS * CH), lambda i, n: (i, 0, 0, 0)),
                pl.BlockSpec((1, DK, MAXCH * HEADS), lambda i, n: (i, 0, 0)),
            ],
        ),
        out_shape=[
            jax.ShapeDtypeStruct((R_DEV, MAXCH, 2 * CH, WIDTH), bf16),
            jax.ShapeDtypeStruct((R_DEV, MAXCH, CH, WIDTH), bf16),
            jax.ShapeDtypeStruct((R_DEV, MAXCH, CH + DK, HEADS * CH), bf16),
            jax.ShapeDtypeStruct((R_DEV, DK, MAXCH * HEADS), f32),
        ],
        compiler_params=pltpu.CompilerParams(vmem_limit_bytes=24 << 20),
        cost_estimate=pl.CostEstimate(
            flops=800_000_000, bytes_accessed=20_000_000, transcendentals=3_000_000
        ),
        name="prepare",
    )(counts, queries, key_vecs, values, log_decay, write_strength, inverses)


def advance(order, hit_rows, ret_owner, counts, stored, wq, u, lk, d, out_gate, gain):
    per = R_DEV // N_TP

    def quarter_rows(index):
        return pl.BlockSpec(
            (ROWS, WIDTH),
            lambda i, o, s, r, n: (jnp.clip(i - per * index, 0, per - 1), 0),
        )

    return pl.pallas_call(
        advance_kernel,
        grid_spec=pltpu.PrefetchScalarGridSpec(
            num_scalar_prefetch=4,
            grid=(R_DEV,),
            in_specs=[
                pl.BlockSpec((1, HEADS * DK, DV), lambda i, o, s, r, n: (s[o[i]], 0, 0)),
                pl.BlockSpec((1, MAXCH, 2 * CH, WIDTH), lambda i, o, s, r, n: (o[i], 0, 0, 0)),
                pl.BlockSpec((1, MAXCH, CH, WIDTH), lambda i, o, s, r, n: (o[i], 0, 0, 0)),
                pl.BlockSpec(
                    (1, MAXCH, CH + DK, HEADS * CH), lambda i, o, s, r, n: (o[i], 0, 0, 0)
                ),
                pl.BlockSpec((1, DK, MAXCH * HEADS), lambda i, o, s, r, n: (o[i], 0, 0)),
                pl.BlockSpec((ROWS, WIDTH), lambda i, o, s, r, n: (o[i], 0)),
                pl.BlockSpec((1, DV), lambda i, o, s, r, n: (0, 0)),
            ],
            out_specs=[quarter_rows(index) for index in range(N_TP)]
            + [pl.BlockSpec((1, HEADS * DK, DV), lambda i, o, s, r, n: (r[o[i]], 0, 0))],
            scratch_shapes=[pltpu.VMEM((ROWS, WIDTH), bf16)],
        ),
        out_shape=[jax.ShapeDtypeStruct((per * ROWS, WIDTH), bf16)] * N_TP
        + [jax.ShapeDtypeStruct((CACHE, HEADS * DK, DV), bf16)],
        compiler_params=pltpu.CompilerParams(vmem_limit_bytes=24 << 20),
        cost_estimate=pl.CostEstimate(
            flops=1_000_000_000, bytes_accessed=18_000_000, transcendentals=2_000_000
        ),
        name="advance",
    )(order, hit_rows, ret_owner, counts, stored, wq, u, lk, d, out_gate, gain)


def project(core, gated, own_weight, direct, swapped):
    tiles = 3
    tile = HALF // tiles
    rows = gated[0].shape[0]
    whole = pl.BlockSpec((rows, WIDTH), lambda j, t, c: (0, 0))
    chosen = lambda j, c: jnp.where(j == 0, c[0], 1 - c[0])
    return pl.pallas_call(
        project_kernel,
        grid_spec=pltpu.PrefetchScalarGridSpec(
            num_scalar_prefetch=1,
            grid=(2, tiles),
            in_specs=[whole] * 4
            + [pl.BlockSpec((WIDTH, tile), lambda j, t, c: (0, chosen(j, c) * tiles + t))]
            + [pl.BlockSpec((WIDTH, tile), lambda j, t, c: (0, jnp.where(j == 0, t, tiles - 1)))]
            * 3
            + [pl.BlockSpec((WIDTH, tile), lambda j, t, c: (0, jnp.where(j == 0, 0, t)))] * 3,
            out_specs=pl.BlockSpec((rows, tile), lambda j, t, c: (0, chosen(j, c) * tiles + t)),
        ),
        out_shape=jax.ShapeDtypeStruct((rows, D), bf16),
        compiler_params=pltpu.CompilerParams(vmem_limit_bytes=24 << 20),
        cost_estimate=pl.CostEstimate(
            flops=4_800_000_000, bytes_accessed=14_000_000, transcendentals=0
        ),
        name="project",
    )(core, *gated, own_weight, *direct, *swapped)


def unpack(source, received):
    return pl.pallas_call(
        unpack_kernel,
        grid_spec=pltpu.PrefetchScalarGridSpec(
            num_scalar_prefetch=1,
            grid=(R_DEV,),
            in_specs=[pl.BlockSpec((1, HEADS * DK, DV), lambda i, s: (s[i], 0, 0))],
            out_specs=pl.BlockSpec((1, HEADS * DK, DV), lambda i, s: (i, 0, 0)),
        ),
        out_shape=jax.ShapeDtypeStruct((R_DEV, HEADS * DK, DV), f32),
        compiler_params=pltpu.CompilerParams(vmem_limit_bytes=16 << 20),
        cost_estimate=pl.CostEstimate(flops=0, bytes_accessed=6_300_000, transcendentals=0),
        name="unpack",
    )(source, received)


def along_tp(x, shift):
    return lax.ppermute(x, "tp", [(z, (z + shift) % N_TP) for z in range(N_TP)])


def to_sibling(x):
    return lax.ppermute(x, "cache", [(i, i ^ 1) for i in range(CACHE)])


def body(
    queries,
    key_vecs,
    values,
    log_decay,
    write_strength,
    inverses,
    suffix_stretches,
    ckpt_store,
    hit_owner,
    hit_slot,
    ret_owner,
    out_gate,
    norm_gain,
    out_weight,
):
    self_index = lax.axis_index("cache")
    z = lax.axis_index("tp")
    core = lax.rem(self_index, 2)
    stored_here = ckpt_store.shape[0]

    tags = jnp.zeros((stored_here, TAG_ROWS, DV), bf16)
    tags = tags.at[:, 0, :R_DEV].set(ret_owner.astype(bf16)[None])
    stored = jnp.concatenate(
        [ckpt_store.astype(bf16).reshape(stored_here, HEADS * DK, DV), tags], axis=1
    )
    stored = lax.all_gather(stored, "cache", axis=0, tiled=True)

    half_weight = lax.dynamic_slice(out_weight, (0, core * HALF), (WIDTH, HALF))
    shifts = QUARTER_SHIFTS[:3]
    direct = [along_tp(half_weight, shift) for shift in shifts]

    wq, u, lk, d = prepare(
        suffix_stretches, queries, key_vecs, values, log_decay, write_strength, inverses
    )

    place = jnp.arange(R_DEV, dtype=jnp.int32)
    per = R_DEV // N_TP
    turn = jnp.repeat(jnp.asarray(QUARTER_SHIFTS, jnp.int32), per)
    order = lax.rem(z + turn, N_TP) * per + lax.rem(place, per)
    hit_rows = hit_owner * stored_here + hit_slot
    *gated, sending = advance(
        order,
        hit_rows,
        ret_owner,
        suffix_stretches,
        stored,
        wq,
        u,
        lk,
        d,
        out_gate,
        norm_gain.reshape(1, DV),
    )
    received = lax.all_to_all(sending, "cache", split_axis=0, concat_axis=0, tiled=True)

    others = [along_tp(rows, shift) for rows, shift in zip(gated[:3], shifts)]
    swapped = [to_sibling(weight) for weight in direct]
    mixed = project(core.reshape(1), others + [gated[3]], out_weight, direct, swapped)

    owners = stored[::stored_here, HEADS * DK, :R_DEV].astype(jnp.int32)
    source = jnp.sum(
        jnp.where(owners == self_index, jnp.arange(CACHE, dtype=jnp.int32)[:, None], 0), axis=0
    )
    new_ckpts = unpack(source, received).reshape(R_DEV, HEADS, DK, DV)
    return (mixed, new_ckpts)


def solution(mesh):
    placed = (
        P("cache", "tp"),
        P("cache", "tp"),
        P("cache", "tp"),
        P("cache", "tp"),
        P("cache", "tp"),
        P("cache", None, "tp"),
        P("cache"),
        P("cache", "tp", None, None),
        P("cache"),
        P("cache"),
        P("cache"),
        P("cache", "tp"),
        P(),
        P("tp", None),
    )
    return jax.shard_map(
        body,
        mesh=mesh,
        in_specs=placed,
        out_specs=(P(("cache", "tp"), None), P("cache", "tp", None, None)),
        check_vma=False,
    )
```

```python
import functools

import jax
import jax.numpy as jnp
from jax import lax
from jax.experimental import pallas as pl
from jax.experimental.pallas import tpu as pltpu
from jax.sharding import PartitionSpec as P

DK = 128
DV = 128
CH = 64
MAXCH = 2
R_DEV = 16
HEADS = 4
PAIRS = HEADS // 2
CACHE = 32
N_TP = 4
CHIP_SHIFTS = (2, 1, 3)
D = 2304
HALF = D // 2
PAIR = 2 * DK
ROWS = MAXCH * CH
TAG_ROWS = 16
READY = 2
GROUP = 4
UNPACKED = 4
VMEM_BYTES = 60 << 20
QUARTER_SHIFTS = (2, 1, 3, 0)

f32 = jnp.float32
bf16 = jnp.bfloat16


def block_diagonal(left, right):
    zeros = jnp.zeros_like(left)
    return jnp.concatenate(
        [jnp.concatenate([left, zeros], axis=1), jnp.concatenate([zeros, right], axis=1)],
        axis=0,
    )


def pair_diagonal(pair):
    return block_diagonal(pair[:, :DK], pair[:, DK:])


def side_by_side(left, right):
    return jnp.concatenate([left, right], axis=1)


def prepare_kernel(
    pair,
    q_ref,
    k_ref,
    v_ref,
    g_ref,
    b_ref,
    m_ref,
    gate_ref,
    gain_ref,
    wq_ref,
    u_ref,
    lk_ref,
    d_ref,
    gain_out_ref,
    decay_ref,
):
    step = pl.program_id(0)
    lower = lax.broadcasted_iota(jnp.int32, (CH, CH), 0) >= lax.broadcasted_iota(
        jnp.int32, (CH, CH), 1
    )
    summing = jnp.where(lower, 1.0, 0.0).astype(bf16)
    row = lax.broadcasted_iota(jnp.int32, (CH, 2 * CH), 0)
    column = lax.broadcasted_iota(jnp.int32, (CH, 2 * CH), 1)
    causal = row >= lax.rem(column, CH)
    first_half = column[:1] < CH
    gain = gain_ref[...]
    decays = []
    for r in range(READY):
        strengths = [
            b_ref[2 * pair + side : 2 * pair + side + 1, pl.ds(r * ROWS, ROWS)]
            for side in range(2)
        ]
        turned = [pltpu.roll(strength, CH, 1) for strength in strengths]
        for c in range(MAXCH):
            rows = pl.ds(r * ROWS + c * CH, CH)
            cumulative = jnp.dot(summing, g_ref[rows, :], preferred_element_type=f32)
            query_fwd, key_fwd, key_back, key_end, plain_values = [], [], [], [], []
            for side in range(2):
                lanes = pl.ds(side * DK, DK)
                q = q_ref[rows, lanes].astype(f32)
                k = k_ref[rows, lanes].astype(f32)
                cum = cumulative[:, side * DK : (side + 1) * DK]
                last = cum[CH - 1 : CH, :]
                forward = jnp.exp(cum)
                q_scale = lax.rsqrt(jnp.sum(q * q, axis=1, keepdims=True) + 1e-06)
                k_unit = k * lax.rsqrt(jnp.sum(k * k, axis=1, keepdims=True) + 1e-06)
                query_fwd.append((q * q_scale * forward).astype(bf16))
                key_fwd.append((k_unit * forward).astype(bf16))
                key_back.append((k_unit * jnp.exp(-cum)).astype(bf16))
                key_end.append(k_unit * jnp.exp(last - cum))
                plain_values.append(v_ref[rows, lanes])
                decays.append(jnp.exp(last))
                gate = jax.nn.sigmoid(gate_ref[rows, lanes].astype(f32))
                gain_out_ref[rows, lanes] = (gain * gate).astype(bf16)
            if c == 0:
                strength = jnp.where(first_half, strengths[0], turned[1])
            else:
                strength = jnp.where(first_half, turned[0], strengths[1])
            inverse = (m_ref[r * MAXCH + c] * strength).astype(bf16)
            w = jnp.dot(inverse, block_diagonal(*key_fwd), preferred_element_type=f32)
            u = jnp.dot(inverse, block_diagonal(*plain_values), preferred_element_type=f32)
            queries = side_by_side(*query_fwd)
            scores = lax.dot_general(
                queries,
                block_diagonal(*key_back),
                (((1,), (1,)), ((), ())),
                preferred_element_type=f32,
            )
            wq_ref[r, c, pl.ds(0, CH), :] = w.astype(bf16)
            wq_ref[r, c, pl.ds(CH, CH), :] = queries
            u_ref[r, c] = u.astype(bf16)
            lk_ref[r, c, pl.ds(0, CH), :] = jnp.where(causal, scores, 0.0).astype(bf16)
            lk_ref[r, c, pl.ds(CH, DK), :] = jnp.concatenate(key_end, axis=0).T.astype(bf16)
    decay_ref[pl.ds(pl.multiple_of(step * READY * 4, 8), READY * 4), :] = jnp.concatenate(
        decays, axis=0
    )

    @pl.when(step == R_DEV // READY - 1)
    def _():
        d_ref[...] = decay_ref[...].T


def advance_kernel(
    order_ref,
    place_ref,
    row_ref,
    ret_ref,
    counts_ref,
    *refs,
):
    sources, refs = refs[:-22], refs[-22:]
    ready, gated_outs, send_ref = refs[:5], refs[5:9], refs[9]
    wq_ref, u_ref, lk_ref, d_ref, gain_ref, initial_ref, gated_ref, final_ref = refs[10:18]
    ready_sems, in_sems, gated_sems, out_sems = refs[18:]

    def request_of(place):
        return order_ref[place // GROUP] * GROUP + place % GROUP

    def ready_copies(quarter):
        at = pl.ds(order_ref[quarter] * GROUP, GROUP)
        tokens = pl.ds(order_ref[quarter] * GROUP * ROWS, GROUP * ROWS)
        where = (at, at, at, tokens)
        sources = (ready[0], ready[1], ready[2], ready[4])
        return [
            pltpu.make_async_copy(
                source.at[where[n]], target.at[quarter], ready_sems.at[quarter * 4 + n]
            )
            for n, (source, target) in enumerate(zip(sources, (wq_ref, u_ref, lk_ref, gain_ref)))
        ]

    def decay_copy():
        return pltpu.make_async_copy(ready[3], d_ref, ready_sems.at[N_TP * 4])

    def copy_in(place, side, source):
        row = row_ref[request_of(place) * 2 + side]
        first = 0 if len(sources) > 1 else side * DK
        return pltpu.make_async_copy(
            source.at[row, pl.ds(first, DK)],
            initial_ref.at[place, pl.ds(side * DK, DK)],
            in_sems.at[place * 2 + side],
        )

    def copy_out(place):
        return pltpu.make_async_copy(
            final_ref.at[place], send_ref.at[ret_ref[request_of(place)]], out_sems.at[place]
        )

    def start_states(quarter):
        for place in range(quarter * GROUP, (quarter + 1) * GROUP):
            for side in range(2):
                chosen = place_ref[request_of(place) * 2 + side]
                for index, source in enumerate(sources):

                    @pl.when(chosen == index)
                    def _(place=place, side=side, source=source):
                        copy_in(place, side, source).start()

    def stretch(quarter, c, states, diagonals, decays):
        reads = [
            jnp.dot(wq_ref[quarter, r, c], diagonals[r], preferred_element_type=f32)
            for r in range(GROUP)
        ]
        news = [
            (u_ref[quarter, r, c].astype(f32) - reads[r][:CH]).astype(bf16) for r in range(GROUP)
        ]
        writes = [
            jnp.dot(lk_ref[quarter, r, c], pair_diagonal(news[r]), preferred_element_type=f32)
            for r in range(GROUP)
        ]
        after = []
        for r in range(GROUP):
            sides = []
            for side in range(2):
                at = r * 4 + 2 * c + side
                lanes = slice(side * DV, (side + 1) * DV)
                decay = decays[:, at : at + 1]
                sides.append(decay * states[r][side] + writes[r][CH:, lanes])
            after.append(sides)
        return [reads[r][CH:] + writes[r][:CH] for r in range(GROUP)], after

    def put_gated(quarter, c, outs, lives):
        for r in range(GROUP):
            for side in range(2):
                rows, lanes = pl.ds(r * ROWS + c * CH, CH), pl.ds(side * DV, DV)
                head_out = outs[r][:, side * DV : (side + 1) * DV]
                mean_square = jnp.mean(head_out * head_out, axis=1, keepdims=True)
                gated = head_out * lax.rsqrt(mean_square + 1e-05)
                gated = gated * gain_ref[quarter, rows, lanes].astype(f32)
                if c > 0:
                    gated = jnp.where(lives[r], gated, 0.0)
                gated_ref[quarter, rows, lanes] = gated.astype(bf16)

    decay_copy().start()
    for quarter in range(N_TP):
        start_states(quarter)
        for copy in ready_copies(quarter):
            copy.start()
    decay_copy().wait()

    for quarter in range(N_TP):
        places = [quarter * GROUP + r for r in range(GROUP)]
        lives = [counts_ref[request_of(place)] > 1 for place in places]
        for copy in ready_copies(quarter):
            copy.wait()
        for place in places:
            for side in range(2):
                copy_in(place, side, sources[0]).wait()
        stored = [
            [initial_ref[place, pl.ds(side * DK, DK), :] for side in range(2)] for place in places
        ]
        states = [[side.astype(f32) for side in sides] for sides in stored]
        decays = pltpu.roll(d_ref[...], DK - order_ref[quarter] * GROUP * 4, 1)
        outs, states = stretch(
            quarter, 0, states, [block_diagonal(*sides) for sides in stored], decays
        )
        put_gated(quarter, 0, outs, lives)
        diagonals = [block_diagonal(*[side.astype(bf16) for side in sides]) for sides in states]
        outs, after = stretch(quarter, 1, states, diagonals, decays)
        for r, place in enumerate(places):
            for side in range(2):
                final = jnp.where(lives[r], after[r][side], states[r][side])
                final_ref[place, pl.ds(side * DK, DK), :] = final.astype(bf16)
            copy_out(place).start()
        put_gated(quarter, 1, outs, lives)
        pltpu.make_async_copy(
            gated_ref.at[quarter], gated_outs[quarter], gated_sems.at[quarter]
        ).start()

    for quarter in range(N_TP):
        pltpu.make_async_copy(
            gated_ref.at[quarter], gated_outs[quarter], gated_sems.at[quarter]
        ).wait()
    for place in range(R_DEV):
        copy_out(place).wait()


def pack_kernel(core_ref, owner_ref, store_ref, keep_ref, give_ref, later_ref):
    core = core_ref[0]
    lane = lax.broadcasted_iota(jnp.int32, (TAG_ROWS, DV), 1)
    tag = jnp.zeros((TAG_ROWS, DV), jnp.int32)
    for r in range(R_DEV):
        tag = jnp.where(lane == r, owner_ref[r], tag)
    tag = tag.astype(f32).astype(bf16)
    for row in range(later_ref.shape[0]):
        keep_ref[row] = store_ref[row, core].astype(bf16)
        give_ref[row] = store_ref[row, 1 - core].astype(bf16)
        for side in range(2):
            later_ref[row, pl.ds(side * DK, DK), :] = store_ref[row, 2 + side].astype(bf16)
        later_ref[row, pl.ds(PAIR, TAG_ROWS), :] = tag


def locate_kernel(self_ref, tag_ref, source_ref):
    self_owner = self_ref[0].astype(f32)
    source = jnp.zeros((1, DV), f32)
    for block in range(CACHE):
        named = tag_ref[block].astype(f32)[:1, :] == self_owner
        source = source + jnp.where(named, float(block), 0.0)
    source_ref[...] = source.astype(jnp.int32)


def project_kernel(core_ref, *refs):
    gated, own_ref, direct, swapped = refs[:8], refs[8], refs[9:13], refs[13:17]
    out_ref = refs[17]

    def total(weights):
        acc = None
        for p in range(PAIRS):
            rows = pl.ds(p * PAIR, PAIR)
            sides = [weights[p][...]] + [ref[rows, :] for ref in (*weights[2:], own_ref)]
            for rows_ref, side in zip(gated[p * N_TP : (p + 1) * N_TP], sides):
                part = jnp.dot(rows_ref[...], side, preferred_element_type=f32)
                acc = part if acc is None else acc + part
        return acc.astype(bf16)

    @pl.when(pl.program_id(0) == 0)
    def _():
        out_ref[...] = total(direct)

    @pl.when(pl.program_id(0) == 1)
    def _():
        out_ref[...] = total(swapped)


def unpack_kernel(source_ref, *refs):
    for place in range(UNPACKED):
        refs[-1][place] = refs[place][0].astype(f32)


def pack(core, owners, ckpt_store):
    stored_here = ckpt_store.shape[0]
    whole = pl.BlockSpec(memory_space=pltpu.VMEM)
    scalars = pl.BlockSpec(memory_space=pltpu.SMEM)
    return pl.pallas_call(
        pack_kernel,
        in_specs=[scalars, scalars, whole],
        out_shape=[
            jax.ShapeDtypeStruct((stored_here, DK, DV), bf16),
            jax.ShapeDtypeStruct((stored_here, DK, DV), bf16),
            jax.ShapeDtypeStruct((stored_here, PAIR + TAG_ROWS, DV), bf16),
        ],
        compiler_params=pltpu.CompilerParams(vmem_limit_bytes=VMEM_BYTES),
        cost_estimate=pl.CostEstimate(flops=0, bytes_accessed=800_000, transcendentals=0),
        name="pack",
    )(core, owners, ckpt_store)


def locate(self_index, gathered):
    return pl.pallas_call(
        locate_kernel,
        grid=(1,),
        in_specs=[
            pl.BlockSpec(memory_space=pltpu.SMEM),
            pl.BlockSpec((CACHE, TAG_ROWS, DV), lambda i: (0, PAIR // TAG_ROWS, 0)),
        ],
        out_specs=pl.BlockSpec((1, DV), lambda i: (0, 0)),
        out_shape=jax.ShapeDtypeStruct((1, DV), jnp.int32),
        compiler_params=pltpu.CompilerParams(vmem_limit_bytes=VMEM_BYTES),
        cost_estimate=pl.CostEstimate(flops=0, bytes_accessed=200_000, transcendentals=0),
        name="locate",
    )(self_index, gathered.reshape(CACHE, -1, DV)).reshape(DV)


def prepare(pair, queries, key_vecs, values, log_decay, write_strength, inverses, out_gate, gain):
    token_rows = pl.BlockSpec((READY * ROWS, PAIR), lambda i: (i, pair))
    return pl.pallas_call(
        functools.partial(prepare_kernel, pair),
        grid=(R_DEV // READY,),
        in_specs=[token_rows] * 4
        + [
            pl.BlockSpec((HEADS, READY * ROWS), lambda i: (0, i)),
            pl.BlockSpec((READY * MAXCH, CH, 2 * CH), lambda i: (i, 0, pair)),
            token_rows,
            pl.BlockSpec((1, DV), lambda i: (0, 0)),
        ],
        out_specs=[
            pl.BlockSpec((READY, MAXCH, 2 * CH, PAIR), lambda i: (i, 0, 0, 0)),
            pl.BlockSpec((READY, MAXCH, CH, PAIR), lambda i: (i, 0, 0, 0)),
            pl.BlockSpec((READY, MAXCH, CH + DK, 2 * CH), lambda i: (i, 0, 0, 0)),
            pl.BlockSpec((DK, DK), lambda i: (0, 0)),
            pl.BlockSpec((READY * ROWS, PAIR), lambda i: (i, 0)),
        ],
        out_shape=[
            jax.ShapeDtypeStruct((R_DEV, MAXCH, 2 * CH, PAIR), bf16),
            jax.ShapeDtypeStruct((R_DEV, MAXCH, CH, PAIR), bf16),
            jax.ShapeDtypeStruct((R_DEV, MAXCH, CH + DK, 2 * CH), bf16),
            jax.ShapeDtypeStruct((DK, DK), f32),
            jax.ShapeDtypeStruct((R_DEV * ROWS, PAIR), bf16),
        ],
        scratch_shapes=[pltpu.VMEM((DK, DK), f32)],
        compiler_params=pltpu.CompilerParams(vmem_limit_bytes=VMEM_BYTES),
        cost_estimate=pl.CostEstimate(
            flops=400_000_000, bytes_accessed=14_000_000, transcendentals=2_000_000
        ),
        name="prepare",
    )(queries, key_vecs, values, log_decay, write_strength.T, inverses, out_gate, gain)


def advance(order, place, row, ret_owner, counts, sources, ready):
    anywhere = pl.BlockSpec(memory_space=pl.ANY)
    return pl.pallas_call(
        advance_kernel,
        grid_spec=pltpu.PrefetchScalarGridSpec(
            num_scalar_prefetch=5,
            grid=(1,),
            in_specs=[anywhere] * (len(sources) + len(ready)),
            out_specs=[anywhere] * (N_TP + 1),
            scratch_shapes=[
                pltpu.VMEM((N_TP, GROUP, MAXCH, 2 * CH, PAIR), bf16),
                pltpu.VMEM((N_TP, GROUP, MAXCH, CH, PAIR), bf16),
                pltpu.VMEM((N_TP, GROUP, MAXCH, CH + DK, 2 * CH), bf16),
                pltpu.VMEM((DK, DK), f32),
                pltpu.VMEM((N_TP, GROUP * ROWS, PAIR), bf16),
                pltpu.VMEM((R_DEV, PAIR, DV), bf16),
                pltpu.VMEM((N_TP, GROUP * ROWS, PAIR), bf16),
                pltpu.VMEM((R_DEV, PAIR, DV), bf16),
                pltpu.SemaphoreType.DMA((N_TP * 4 + 1,)),
                pltpu.SemaphoreType.DMA((R_DEV * 2,)),
                pltpu.SemaphoreType.DMA((N_TP,)),
                pltpu.SemaphoreType.DMA((R_DEV,)),
            ],
        ),
        out_shape=[jax.ShapeDtypeStruct((GROUP * ROWS, PAIR), bf16)] * N_TP
        + [jax.ShapeDtypeStruct((CACHE, PAIR, DV), bf16)],
        compiler_params=pltpu.CompilerParams(vmem_limit_bytes=VMEM_BYTES),
        cost_estimate=pl.CostEstimate(
            flops=500_000_000, bytes_accessed=10_000_000, transcendentals=100_000
        ),
        name="advance",
    )(order, place, row, ret_owner, counts, *sources, *ready)


def project(core, gated, own_weight, direct, swapped):
    tiles = 3
    tile = HALF // tiles
    rows = gated[0].shape[0]
    whole = pl.BlockSpec((rows, PAIR), lambda j, t, c: (0, 0))
    chosen = lambda j, c: jnp.where(j == 0, c[0], 1 - c[0])
    heights = [weight.shape[0] for weight in direct]
    return pl.pallas_call(
        project_kernel,
        grid_spec=pltpu.PrefetchScalarGridSpec(
            num_scalar_prefetch=1,
            grid=(2, tiles),
            in_specs=[whole] * (PAIRS * N_TP)
            + [pl.BlockSpec((HEADS * DK, tile), lambda j, t, c: (0, chosen(j, c) * tiles + t))]
            + [
                pl.BlockSpec((height, tile), lambda j, t, c: (0, jnp.where(j == 0, t, tiles - 1)))
                for height in heights
            ]
            + [
                pl.BlockSpec((height, tile), lambda j, t, c: (0, jnp.where(j == 0, 0, t)))
                for height in heights
            ],
            out_specs=pl.BlockSpec((rows, tile), lambda j, t, c: (0, chosen(j, c) * tiles + t)),
        ),
        out_shape=jax.ShapeDtypeStruct((rows, D), bf16),
        compiler_params=pltpu.CompilerParams(vmem_limit_bytes=VMEM_BYTES),
        cost_estimate=pl.CostEstimate(
            flops=4_800_000_000, bytes_accessed=14_000_000, transcendentals=0
        ),
        name="project",
    )(core, *gated, own_weight, *direct, *swapped)


def unpack(pair, source, received, before=None):
    def slot_of(place):
        return pl.BlockSpec((1, PAIR, DV), lambda i, s: (s[i * UNPACKED + place], 0, 0))

    kept = [] if before is None else [before]
    return pl.pallas_call(
        unpack_kernel,
        grid_spec=pltpu.PrefetchScalarGridSpec(
            num_scalar_prefetch=1,
            grid=(R_DEV // UNPACKED,),
            in_specs=[slot_of(place) for place in range(UNPACKED)]
            + [pl.BlockSpec(memory_space=pl.ANY)] * len(kept),
            out_specs=pl.BlockSpec((UNPACKED, PAIR, DV), lambda i, s: (i, pair, 0)),
        ),
        out_shape=jax.ShapeDtypeStruct((R_DEV, HEADS * DK, DV), f32),
        input_output_aliases={1 + UNPACKED: 0} if kept else {},
        compiler_params=pltpu.CompilerParams(vmem_limit_bytes=VMEM_BYTES),
        cost_estimate=pl.CostEstimate(flops=0, bytes_accessed=3_200_000, transcendentals=0),
        name="unpack",
    )(source, *[received] * UNPACKED, *kept)


def along_tp(x, shift):
    return lax.ppermute(x, "tp", [(z, (z + shift) % N_TP) for z in range(N_TP)])


def chip_and_core(index):
    return index // 8, index // 2 % 4, index % 2


def to_sibling(x):
    return lax.ppermute(x, "cache", [(i, i ^ 1) for i in range(CACHE)])


def along_chips(x, turned, shift):
    pairs = []
    for index in range(CACHE):
        chip_x, chip_y, core = chip_and_core(index)
        if (core == 0) != turned:
            chip_x = (chip_x + shift) % 4
        else:
            chip_y = (chip_y + shift) % 4
        pairs.append((index, (chip_x * 4 + chip_y) * 2 + core))
    return lax.ppermute(x, "cache", pairs)


def gather_by_chips(keep, give, beside, work):
    mine = jnp.concatenate([keep, to_sibling(give)], axis=0)
    line = jnp.concatenate(
        [mine] + [along_chips(mine, False, shift) for shift in CHIP_SHIFTS], axis=0
    )
    line, tokens = lax.optimization_barrier((line, beside[0]))
    beside = (tokens, beside[1])
    plane = [line] + [along_chips(line, True, shift) for shift in CHIP_SHIFTS]
    plane, done = lax.optimization_barrier((plane, work(beside)))
    return plane + [to_sibling(part) for part in plane], done


def places_by_chips(self_index, owner, slot):
    here_x, here_y, here_core = chip_and_core(self_index)
    chip_x, chip_y, core = chip_and_core(owner)
    ordinal = jnp.asarray([0, 2, 1, 3], jnp.int32)
    away_x = ordinal[lax.rem(here_x - chip_x + 4, 4)]
    away_y = ordinal[lax.rem(here_y - chip_y + 4, 4)]
    places, rows = [], []
    for head in range(2):
        first, second = (away_x, away_y) if head == 0 else (away_y, away_x)
        places.append(second + jnp.where(here_core == head, 0, 4))
        rows.append(first * 4 + jnp.where(core == head, 0, 2) + slot)
    return jnp.stack(places, axis=1).reshape(-1), jnp.stack(rows, axis=1).reshape(-1)


def body(
    queries,
    key_vecs,
    values,
    log_decay,
    write_strength,
    inverses,
    suffix_stretches,
    ckpt_store,
    hit_owner,
    hit_slot,
    ret_owner,
    out_gate,
    norm_gain,
    out_weight,
):
    self_index = lax.axis_index("cache").astype(jnp.int32)
    z = lax.axis_index("tp").astype(jnp.int32)
    core = lax.rem(self_index, 2)
    stored_here = ckpt_store.shape[0]

    keep, give, later = pack(core.reshape(1), ret_owner, ckpt_store)
    later = lax.all_gather(later, "cache", axis=0, tiled=True)

    half_weight = lax.dynamic_slice(out_weight, (0, core * HALF), (HEADS * DK, HALF))
    shifts = QUARTER_SHIFTS[:3]
    near_weights = [along_tp(half_weight, shift) for shift in shifts[1:]]

    tokens = (
        queries,
        key_vecs,
        values,
        log_decay,
        write_strength,
        inverses,
        out_gate,
        norm_gain.reshape(1, DV),
    )
    earlier, (ready, near_weights) = gather_by_chips(
        keep,
        give,
        (tokens, near_weights),
        lambda beside: (prepare(0, *beside[0]), beside[1]),
    )

    far_weight = [
        along_tp(weight[p * PAIR : (p + 1) * PAIR], shift)
        for p, (weight, shift) in enumerate(zip(near_weights, shifts[1:]))
    ]

    order = lax.rem(z + jnp.asarray(QUARTER_SHIFTS, jnp.int32), N_TP)
    place, row = places_by_chips(self_index, hit_owner, hit_slot)
    *gated, sending = advance(order, place, row, ret_owner, suffix_stretches, earlier, ready)
    received = [lax.all_to_all(sending, "cache", split_axis=0, concat_axis=0, tiled=True)]
    others = [along_tp(rows, shift) for rows, shift in zip(gated[:3], shifts)]
    gated_parts = others + [gated[3]]

    tokens, _ = lax.optimization_barrier((tokens, sending))
    ready = prepare(1, *tokens)
    later, far_weight, _ = lax.optimization_barrier((later, far_weight, others))
    place = jnp.zeros_like(place)
    row = jnp.repeat(hit_owner * stored_here + hit_slot, 2)
    *gated, sending = advance(order, place, row, ret_owner, suffix_stretches, [later], ready)
    received.append(lax.all_to_all(sending, "cache", split_axis=0, concat_axis=0, tiled=True))
    gated_parts += [along_tp(rows, shift) for rows, shift in zip(gated[:3], shifts)] + [gated[3]]

    direct = [*far_weight, *near_weights]
    swapped = [to_sibling(weight) for weight in direct]
    mixed = project(core.reshape(1), gated_parts, out_weight, direct, swapped)

    source = locate(self_index.reshape(1), later)
    new_ckpts = None
    for p in range(PAIRS):
        new_ckpts = unpack(p, source, received[p], new_ckpts)
    new_ckpts = new_ckpts.reshape(R_DEV, HEADS, DK, DV)
    return (mixed, new_ckpts)


def solution(mesh):
    placed = (
        P("cache", "tp"),
        P("cache", "tp"),
        P("cache", "tp"),
        P("cache", "tp"),
        P("cache", "tp"),
        P("cache", None, "tp"),
        P("cache"),
        P("cache", "tp", None, None),
        P("cache"),
        P("cache"),
        P("cache"),
        P("cache", "tp"),
        P(),
        P("tp", None),
    )
    return jax.shard_map(
        body,
        mesh=mesh,
        in_specs=placed,
        out_specs=(P(("cache", "tp"), None), P("cache", "tp", None, None)),
        check_vma=False,
    )
```

```python
import functools

import jax
import jax.numpy as jnp
from jax import lax
from jax.experimental import pallas as pl
from jax.experimental.pallas import tpu as pltpu
from jax.sharding import PartitionSpec as P

DK = 128
DV = 128
CH = 64
MAXCH = 2
R_DEV = 16
HEADS = 4
PAIRS = HEADS // 2
CACHE = 32
N_TP = 4
CK_DEV = 2
CHIP_SHIFTS = (2, 1, 3)
D = 2304
TILES = 3
PAIR = 2 * DK
ROWS = MAXCH * CH
TAG_ROWS = 16
READY = 4
GROUP = 4
VMEM_BYTES = 60 << 20
UNPACK_BYTES = 8 << 20
QUARTER_SHIFTS = (2, 1, 3, 0)

f32 = jnp.float32
bf16 = jnp.bfloat16


def chip_and_core(index):
    return index // 8, index // 2 % 4, index % 2


def chip_ordinal(shift):
    return jnp.where(shift == 1, 2, jnp.where(shift == 2, 1, shift))


def block_diagonal(left, right):
    zeros = jnp.zeros_like(left)
    return jnp.concatenate(
        [jnp.concatenate([left, zeros], axis=1), jnp.concatenate([zeros, right], axis=1)],
        axis=0,
    )


def pair_diagonal(pair):
    return block_diagonal(pair[:, :DK], pair[:, DK:])


def side_by_side(left, right):
    return jnp.concatenate([left, right], axis=1)


def prepare_kernel(
    pair,
    q_ref,
    k_ref,
    v_ref,
    g_ref,
    b_ref,
    m_ref,
    gate_ref,
    gain_ref,
    wq_ref,
    u_ref,
    lk_ref,
    d_ref,
    gain_out_ref,
    decay_ref,
):
    step = pl.program_id(0)
    lower = lax.broadcasted_iota(jnp.int32, (CH, CH), 0) >= lax.broadcasted_iota(
        jnp.int32, (CH, CH), 1
    )
    summing = jnp.where(lower, 1.0, 0.0).astype(bf16)
    row = lax.broadcasted_iota(jnp.int32, (CH, 2 * CH), 0)
    column = lax.broadcasted_iota(jnp.int32, (CH, 2 * CH), 1)
    causal = row >= lax.rem(column, CH)
    first_half = column[:1] < CH
    gain = gain_ref[...]
    decays = []
    for r in range(READY):
        strengths = [
            b_ref[2 * pair + side : 2 * pair + side + 1, pl.ds(r * ROWS, ROWS)]
            for side in range(2)
        ]
        turned = [pltpu.roll(strength, CH, 1) for strength in strengths]
        for c in range(MAXCH):
            rows = pl.ds(r * ROWS + c * CH, CH)
            cumulative = jnp.dot(summing, g_ref[rows, :], preferred_element_type=f32)
            query_fwd, key_fwd, key_back, key_end, plain_values = [], [], [], [], []
            for side in range(2):
                lanes = pl.ds(side * DK, DK)
                q = q_ref[rows, lanes].astype(f32)
                k = k_ref[rows, lanes].astype(f32)
                cum = cumulative[:, side * DK : (side + 1) * DK]
                last = cum[CH - 1 : CH, :]
                forward = jnp.exp(cum)
                q_scale = lax.rsqrt(jnp.sum(q * q, axis=1, keepdims=True) + 1e-06)
                k_unit = k * lax.rsqrt(jnp.sum(k * k, axis=1, keepdims=True) + 1e-06)
                query_fwd.append((q * q_scale * forward).astype(bf16))
                key_fwd.append((k_unit * forward).astype(bf16))
                key_back.append((k_unit * jnp.exp(-cum)).astype(bf16))
                key_end.append(k_unit * jnp.exp(last - cum))
                plain_values.append(v_ref[rows, lanes])
                decays.append(jnp.exp(last))
                gate = jax.nn.sigmoid(gate_ref[rows, lanes].astype(f32))
                gain_out_ref[rows, lanes] = (gain * gate).astype(bf16)
            if c == 0:
                strength = jnp.where(first_half, strengths[0], turned[1])
            else:
                strength = jnp.where(first_half, turned[0], strengths[1])
            inverse = (m_ref[r * MAXCH + c] * strength).astype(bf16)
            w = jnp.dot(inverse, block_diagonal(*key_fwd), preferred_element_type=f32)
            u = jnp.dot(inverse, block_diagonal(*plain_values), preferred_element_type=f32)
            queries = side_by_side(*query_fwd)
            scores = lax.dot_general(
                queries,
                block_diagonal(*key_back),
                (((1,), (1,)), ((), ())),
                preferred_element_type=f32,
            )
            wq_ref[r, c, pl.ds(0, CH), :] = w.astype(bf16)
            wq_ref[r, c, pl.ds(CH, CH), :] = queries
            u_ref[r, c] = u.astype(bf16)
            lk_ref[r, c, pl.ds(0, CH), :] = jnp.where(causal, scores, 0.0).astype(bf16)
            lk_ref[r, c, pl.ds(CH, DK), :] = jnp.concatenate(key_end, axis=0).T.astype(bf16)
    decay_ref[pl.ds(pl.multiple_of(step * READY * 4, 8), READY * 4), :] = jnp.concatenate(
        decays, axis=0
    )

    @pl.when(step == R_DEV // READY - 1)
    def _():
        d_ref[...] = decay_ref[...].T


def advance_kernel(
    owner_ref,
    slot_ref,
    ret_ref,
    counts_ref,
    *refs,
):
    sources, refs = refs[:-22], refs[-22:]
    ready, gated_outs, send_ref = refs[:5], refs[5:9], refs[9]
    wq_ref, u_ref, lk_ref, d_ref, gain_ref, initial_ref, gated_ref, final_ref = refs[10:18]
    ready_sems, in_sems, gated_sems, out_sems = refs[18:]

    here_x, here_y, here_core = chip_and_core(lax.axis_index("cache"))
    z = lax.axis_index("tp")
    order = [lax.rem(z + shift, N_TP) for shift in QUARTER_SHIFTS]

    def request_of(place):
        return order[place // GROUP] * GROUP + place % GROUP

    def whereabouts(place):
        owner, slot = owner_ref[request_of(place)], slot_ref[request_of(place)]
        if len(sources) == 1:
            return 0, owner * CK_DEV + slot
        chip_x, chip_y, core = chip_and_core(owner)
        away_x = chip_ordinal(lax.rem(here_x - chip_x + 4, 4))
        away_y = chip_ordinal(lax.rem(here_y - chip_y + 4, 4))
        first = jnp.where(core == 0, away_x, away_y)
        second = jnp.where(core == 0, away_y, away_x)
        return second + jnp.where(core == here_core, 0, 4), first * CK_DEV + slot

    def ready_copies(quarter):
        at = pl.ds(order[quarter] * GROUP, GROUP)
        tokens = pl.ds(order[quarter] * GROUP * ROWS, GROUP * ROWS)
        where = (at, at, at, tokens)
        sources = (ready[0], ready[1], ready[2], ready[4])
        return [
            pltpu.make_async_copy(
                source.at[where[n]], target.at[quarter], ready_sems.at[quarter * 4 + n]
            )
            for n, (source, target) in enumerate(zip(sources, (wq_ref, u_ref, lk_ref, gain_ref)))
        ]

    def decay_copy():
        return pltpu.make_async_copy(ready[3], d_ref, ready_sems.at[N_TP * 4])

    def copy_in(place, source, row):
        return pltpu.make_async_copy(
            source.at[row, pl.ds(0, PAIR)], initial_ref.at[place], in_sems.at[place]
        )

    def copy_out(place):
        return pltpu.make_async_copy(
            final_ref.at[place], send_ref.at[ret_ref[request_of(place)]], out_sems.at[place]
        )

    def start_states(quarter):
        for place in range(quarter * GROUP, (quarter + 1) * GROUP):
            chosen, row = whereabouts(place)
            for index, source in enumerate(sources):

                @pl.when(chosen == index)
                def _(place=place, source=source, row=row):
                    copy_in(place, source, row).start()

    def stretch(quarter, c, states, diagonals, decays):
        reads = [
            jnp.dot(wq_ref[quarter, r, c], diagonals[r], preferred_element_type=f32)
            for r in range(GROUP)
        ]
        news = [
            (u_ref[quarter, r, c].astype(f32) - reads[r][:CH]).astype(bf16) for r in range(GROUP)
        ]
        writes = [
            jnp.dot(lk_ref[quarter, r, c], pair_diagonal(news[r]), preferred_element_type=f32)
            for r in range(GROUP)
        ]
        after = []
        for r in range(GROUP):
            sides = []
            for side in range(2):
                at = r * 4 + 2 * c + side
                lanes = slice(side * DV, (side + 1) * DV)
                decay = decays[:, at : at + 1]
                sides.append(decay * states[r][side] + writes[r][CH:, lanes])
            after.append(sides)
        return [reads[r][CH:] + writes[r][:CH] for r in range(GROUP)], after

    def put_gated(quarter, c, outs, lives):
        for r in range(GROUP):
            for side in range(2):
                rows, lanes = pl.ds(r * ROWS + c * CH, CH), pl.ds(side * DV, DV)
                head_out = outs[r][:, side * DV : (side + 1) * DV]
                mean_square = jnp.mean(head_out * head_out, axis=1, keepdims=True)
                gated = head_out * lax.rsqrt(mean_square + 1e-05)
                gated = gated * gain_ref[quarter, rows, lanes].astype(f32)
                if c > 0:
                    gated = jnp.where(lives[r], gated, 0.0)
                gated_ref[quarter, rows, lanes] = gated.astype(bf16)

    decay_copy().start()
    for quarter in range(N_TP):
        for copy in ready_copies(quarter):
            copy.start()
        if quarter < 2:
            start_states(quarter)
    decay_copy().wait()

    for quarter in range(N_TP):
        places = [quarter * GROUP + r for r in range(GROUP)]
        lives = [counts_ref[request_of(place)] > 1 for place in places]
        for copy in ready_copies(quarter):
            copy.wait()
        for place in places:
            copy_in(place, sources[0], 0).wait()
        stored = [
            [initial_ref[place, pl.ds(side * DK, DK), :] for side in range(2)] for place in places
        ]
        states = [[side.astype(f32) for side in sides] for sides in stored]
        decays = pltpu.roll(d_ref[...], DK - order[quarter] * GROUP * 4, 1)
        outs, states = stretch(
            quarter, 0, states, [block_diagonal(*sides) for sides in stored], decays
        )
        put_gated(quarter, 0, outs, lives)
        diagonals = [block_diagonal(*[side.astype(bf16) for side in sides]) for sides in states]
        outs, after = stretch(quarter, 1, states, diagonals, decays)
        for r, place in enumerate(places):
            for side in range(2):
                final = jnp.where(lives[r], after[r][side], states[r][side])
                final_ref[place, pl.ds(side * DK, DK), :] = final.astype(bf16)
            copy_out(place).start()
        put_gated(quarter, 1, outs, lives)
        if quarter + 2 < N_TP:
            start_states(quarter + 2)
        pltpu.make_async_copy(
            gated_ref.at[quarter], gated_outs[quarter], gated_sems.at[quarter]
        ).start()

    for quarter in range(N_TP):
        pltpu.make_async_copy(
            gated_ref.at[quarter], gated_outs[quarter], gated_sems.at[quarter]
        ).wait()
    for place in range(R_DEV):
        copy_out(place).wait()


def pack_kernel(owner_ref, store_ref, earlier_ref, later_ref):
    lane = lax.broadcasted_iota(jnp.int32, (TAG_ROWS, DV), 1)
    tag = jnp.zeros((TAG_ROWS, DV), jnp.int32)
    for r in range(R_DEV):
        tag = jnp.where(lane == r, owner_ref[r], tag)
    tag = tag.astype(f32).astype(bf16)
    for row in range(CK_DEV):
        for side in range(2):
            earlier_ref[row, pl.ds(side * DK, DK), :] = store_ref[row, side].astype(bf16)
            later_ref[row, pl.ds(side * DK, DK), :] = store_ref[row, 2 + side].astype(bf16)
        later_ref[row, pl.ds(PAIR, TAG_ROWS), :] = tag


def locate_kernel(tag_ref, source_ref):
    self_owner = lax.axis_index("cache").astype(f32)
    source = jnp.zeros((1, DV), f32)
    for block in range(CACHE):
        named = tag_ref[block].astype(f32)[:1, :] == self_owner
        source = source + jnp.where(named, float(block), 0.0)
    source_ref[...] = source.astype(jnp.int32)


def project_kernel(*refs):
    gated, own_ref, mine_ref, sibling_ref = refs[:8], refs[8], refs[9], refs[10]
    far_mine_ref, far_sibling_ref, out_ref = refs[11:]
    core = lax.axis_index("cache") % 2
    rows = jnp.concatenate([ref[...] for ref in gated], axis=1)

    def put(below_ref, above_ref, far_refs):
        weights = []
        for p in range(PAIRS):
            at = pl.ds(p * PAIR, PAIR)
            weights += [far_refs[p][...], below_ref[at, :], above_ref[at, :], own_ref[at, :]]
        out_ref[...] = jnp.dot(
            rows, jnp.concatenate(weights, axis=0), preferred_element_type=f32
        ).astype(bf16)

    @pl.when(core == 0)
    def _():
        put(mine_ref, sibling_ref, (far_mine_ref, far_sibling_ref))

    @pl.when(core == 1)
    def _():
        put(sibling_ref, mine_ref, (far_sibling_ref, far_mine_ref))


def unpack_kernel(pair, source_ref, received_ref, *refs):
    out_ref, slots_ref, states_ref, in_sems, out_sems = refs[-5:]

    def copy_in(place):
        return pltpu.make_async_copy(
            received_ref.at[source_ref[place]], slots_ref.at[place], in_sems.at[place]
        )

    def copy_out(place):
        return pltpu.make_async_copy(
            states_ref.at[place],
            out_ref.at[place, pl.ds(pair * PAIR, PAIR)],
            out_sems.at[place],
        )

    for place in range(R_DEV):
        copy_in(place).start()
    for place in range(R_DEV):
        copy_in(place).wait()
        states_ref[place] = slots_ref[place].astype(f32)
        copy_out(place).start()
    for place in range(R_DEV):
        copy_out(place).wait()


def pack(owners, ckpt_store):
    whole = pl.BlockSpec(memory_space=pltpu.VMEM)
    return pl.pallas_call(
        pack_kernel,
        in_specs=[pl.BlockSpec(memory_space=pltpu.SMEM), whole],
        out_shape=[
            jax.ShapeDtypeStruct((CK_DEV, PAIR, DV), bf16),
            jax.ShapeDtypeStruct((CK_DEV, PAIR + TAG_ROWS, DV), bf16),
        ],
        compiler_params=pltpu.CompilerParams(vmem_limit_bytes=VMEM_BYTES),
        cost_estimate=pl.CostEstimate(flops=0, bytes_accessed=800_000, transcendentals=0),
        name="pack",
    )(owners, ckpt_store)


def locate(gathered):
    return pl.pallas_call(
        locate_kernel,
        grid=(1,),
        in_specs=[pl.BlockSpec((CACHE, TAG_ROWS, DV), lambda i: (0, PAIR // TAG_ROWS, 0))],
        out_specs=pl.BlockSpec((1, DV), lambda i: (0, 0)),
        out_shape=jax.ShapeDtypeStruct((1, DV), jnp.int32),
        compiler_params=pltpu.CompilerParams(vmem_limit_bytes=VMEM_BYTES),
        cost_estimate=pl.CostEstimate(flops=0, bytes_accessed=200_000, transcendentals=0),
        name="locate",
    )(gathered.reshape(CACHE, -1, DV)).reshape(DV)


def prepare(pair, queries, key_vecs, values, log_decay, write_strength, inverses, out_gate, gain):
    token_rows = pl.BlockSpec((READY * ROWS, PAIR), lambda i: (i, pair))
    return pl.pallas_call(
        functools.partial(prepare_kernel, pair),
        grid=(R_DEV // READY,),
        in_specs=[token_rows] * 4
        + [
            pl.BlockSpec((HEADS, READY * ROWS), lambda i: (0, i)),
            pl.BlockSpec((READY * MAXCH, CH, 2 * CH), lambda i: (i, 0, pair)),
            token_rows,
            pl.BlockSpec((1, DV), lambda i: (0, 0)),
        ],
        out_specs=[
            pl.BlockSpec((READY, MAXCH, 2 * CH, PAIR), lambda i: (i, 0, 0, 0)),
            pl.BlockSpec((READY, MAXCH, CH, PAIR), lambda i: (i, 0, 0, 0)),
            pl.BlockSpec((READY, MAXCH, CH + DK, 2 * CH), lambda i: (i, 0, 0, 0)),
            pl.BlockSpec((DK, DK), lambda i: (0, 0)),
            pl.BlockSpec((READY * ROWS, PAIR), lambda i: (i, 0)),
        ],
        out_shape=[
            jax.ShapeDtypeStruct((R_DEV, MAXCH, 2 * CH, PAIR), bf16),
            jax.ShapeDtypeStruct((R_DEV, MAXCH, CH, PAIR), bf16),
            jax.ShapeDtypeStruct((R_DEV, MAXCH, CH + DK, 2 * CH), bf16),
            jax.ShapeDtypeStruct((DK, DK), f32),
            jax.ShapeDtypeStruct((R_DEV * ROWS, PAIR), bf16),
        ],
        scratch_shapes=[pltpu.VMEM((DK, DK), f32)],
        compiler_params=pltpu.CompilerParams(vmem_limit_bytes=VMEM_BYTES),
        cost_estimate=pl.CostEstimate(
            flops=400_000_000, bytes_accessed=14_000_000, transcendentals=2_000_000
        ),
        name="prepare",
    )(queries, key_vecs, values, log_decay, write_strength.T, inverses, out_gate, gain)


def advance(hit_owner, hit_slot, ret_owner, counts, sources, ready):
    anywhere = pl.BlockSpec(memory_space=pl.ANY)
    return pl.pallas_call(
        advance_kernel,
        grid_spec=pltpu.PrefetchScalarGridSpec(
            num_scalar_prefetch=4,
            grid=(1,),
            in_specs=[anywhere] * (len(sources) + len(ready)),
            out_specs=[anywhere] * (N_TP + 1),
            scratch_shapes=[
                pltpu.VMEM((N_TP, GROUP, MAXCH, 2 * CH, PAIR), bf16),
                pltpu.VMEM((N_TP, GROUP, MAXCH, CH, PAIR), bf16),
                pltpu.VMEM((N_TP, GROUP, MAXCH, CH + DK, 2 * CH), bf16),
                pltpu.VMEM((DK, DK), f32),
                pltpu.VMEM((N_TP, GROUP * ROWS, PAIR), bf16),
                pltpu.VMEM((R_DEV, PAIR, DV), bf16),
                pltpu.VMEM((N_TP, GROUP * ROWS, PAIR), bf16),
                pltpu.VMEM((R_DEV, PAIR, DV), bf16),
                pltpu.SemaphoreType.DMA((N_TP * 4 + 1,)),
                pltpu.SemaphoreType.DMA((R_DEV,)),
                pltpu.SemaphoreType.DMA((N_TP,)),
                pltpu.SemaphoreType.DMA((R_DEV,)),
            ],
        ),
        out_shape=[jax.ShapeDtypeStruct((GROUP * ROWS, PAIR), bf16)] * N_TP
        + [jax.ShapeDtypeStruct((CACHE, PAIR, DV), bf16)],
        compiler_params=pltpu.CompilerParams(vmem_limit_bytes=VMEM_BYTES),
        cost_estimate=pl.CostEstimate(
            flops=500_000_000, bytes_accessed=10_000_000, transcendentals=100_000
        ),
        name="advance",
    )(hit_owner, hit_slot, ret_owner, counts, *sources, *ready)


def project(gated, own_weight, weights):
    tile = D // TILES
    rows = gated[0].shape[0]
    weights = [own_weight, *weights]
    return pl.pallas_call(
        project_kernel,
        grid=(TILES,),
        in_specs=[pl.BlockSpec((rows, PAIR), lambda t: (0, 0))] * (PAIRS * N_TP)
        + [pl.BlockSpec((weight.shape[0], tile), lambda t: (0, t)) for weight in weights],
        out_specs=pl.BlockSpec((rows, tile), lambda t: (0, t)),
        out_shape=jax.ShapeDtypeStruct((rows, D), bf16),
        compiler_params=pltpu.CompilerParams(vmem_limit_bytes=VMEM_BYTES),
        cost_estimate=pl.CostEstimate(
            flops=4_800_000_000, bytes_accessed=14_000_000, transcendentals=0
        ),
        name="project",
    )(*gated, *weights)


def unpack(pair, source, received, before=None):
    kept = [] if before is None else [before]
    return pl.pallas_call(
        functools.partial(unpack_kernel, pair),
        grid_spec=pltpu.PrefetchScalarGridSpec(
            num_scalar_prefetch=1,
            grid=(1,),
            in_specs=[pl.BlockSpec(memory_space=pl.ANY)] * (1 + len(kept)),
            out_specs=pl.BlockSpec(memory_space=pl.ANY),
            scratch_shapes=[
                pltpu.VMEM((R_DEV, PAIR, DV), bf16),
                pltpu.VMEM((R_DEV, PAIR, DV), f32),
                pltpu.SemaphoreType.DMA((R_DEV,)),
                pltpu.SemaphoreType.DMA((R_DEV,)),
            ],
        ),
        out_shape=jax.ShapeDtypeStruct((R_DEV, HEADS * DK, DV), f32),
        input_output_aliases={2: 0} if kept else {},
        compiler_params=pltpu.CompilerParams(vmem_limit_bytes=UNPACK_BYTES),
        cost_estimate=pl.CostEstimate(flops=0, bytes_accessed=3_200_000, transcendentals=0),
        name="unpack",
    )(source, received, *kept)


def along_tp(x, shift):
    return lax.ppermute(x, "tp", [(z, (z + shift) % N_TP) for z in range(N_TP)])


def by_cores_along_tp(x):
    pairs = []
    for index in range(CACHE):
        for z in range(N_TP):
            to = (z + (1 if index % 2 == 0 else N_TP - 1)) % N_TP
            pairs.append((index * N_TP + z, index * N_TP + to))
    return lax.ppermute(x, ("cache", "tp"), pairs)


def to_sibling(x):
    return lax.ppermute(x, "cache", [(i, i ^ 1) for i in range(CACHE)])


def along_chips(x, turned, shift):
    pairs = []
    for index in range(CACHE):
        chip_x, chip_y, core = chip_and_core(index)
        if (core == 0) != turned:
            chip_x = (chip_x + shift) % 4
        else:
            chip_y = (chip_y + shift) % 4
        pairs.append((index, (chip_x * 4 + chip_y) * 2 + core))
    return lax.ppermute(x, "cache", pairs)


def gather_by_chips(mine, beside, work):
    line = jnp.concatenate(
        [mine] + [along_chips(mine, False, shift) for shift in CHIP_SHIFTS], axis=0
    )
    line, tokens = lax.optimization_barrier((line, beside[0]))
    beside = (tokens, beside[1])
    plane = [along_chips(line, True, shift) for shift in CHIP_SHIFTS]
    plane, done = lax.optimization_barrier((plane, work(beside)))
    plane = [line, *plane]
    return plane + [to_sibling(part) for part in plane], done


def body(
    queries,
    key_vecs,
    values,
    log_decay,
    write_strength,
    inverses,
    suffix_stretches,
    ckpt_store,
    hit_owner,
    hit_slot,
    ret_owner,
    out_gate,
    norm_gain,
    out_weight,
):
    earlier, later = pack(ret_owner, ckpt_store)
    later = lax.all_gather(later, "cache", axis=0, tiled=True)

    near_weight = by_cores_along_tp(out_weight)
    shifts = QUARTER_SHIFTS[:3]

    tokens = (
        queries,
        key_vecs,
        values,
        log_decay,
        write_strength,
        inverses,
        out_gate,
        norm_gain.reshape(1, DV),
    )
    earlier, (ready, near_weight) = gather_by_chips(
        earlier, (tokens, near_weight), lambda beside: (prepare(0, *beside[0]), beside[1])
    )
    core = lax.rem(lax.axis_index("cache"), 2)
    far_weight = by_cores_along_tp(
        lax.dynamic_slice(near_weight, (core * PAIR, 0), (PAIR, D))
    )

    *gated, sending = advance(
        hit_owner, hit_slot, ret_owner, suffix_stretches, earlier, ready
    )
    received = [lax.all_to_all(sending, "cache", split_axis=0, concat_axis=0, tiled=True)]
    others = [along_tp(rows, shift) for rows, shift in zip(gated[:3], shifts)]
    gated_parts = others + [gated[3]]

    tokens, _ = lax.optimization_barrier((tokens, sending))
    ready = prepare(1, *tokens)
    *gated, sending = advance(
        hit_owner, hit_slot, ret_owner, suffix_stretches, [later], ready
    )
    sending, far_weight, _ = lax.optimization_barrier((sending, far_weight, others))
    received.append(lax.all_to_all(sending, "cache", split_axis=0, concat_axis=0, tiled=True))
    gated_parts += [along_tp(rows, shift) for rows, shift in zip(gated[:3], shifts)] + [gated[3]]

    weights = [near_weight, to_sibling(near_weight), far_weight, to_sibling(far_weight)]
    mixed = project(gated_parts, out_weight, weights)

    source = locate(later)
    new_ckpts = None
    for p in range(PAIRS):
        new_ckpts = unpack(p, source, received[p], new_ckpts)
    new_ckpts = new_ckpts.reshape(R_DEV, HEADS, DK, DV)
    return (mixed, new_ckpts)


def solution(mesh):
    placed = (
        P("cache", "tp"),
        P("cache", "tp"),
        P("cache", "tp"),
        P("cache", "tp"),
        P("cache", "tp"),
        P("cache", None, "tp"),
        P("cache"),
        P("cache", "tp", None, None),
        P("cache"),
        P("cache"),
        P("cache"),
        P("cache", "tp"),
        P(),
        P("tp", None),
    )
    return jax.shard_map(
        body,
        mesh=mesh,
        in_specs=placed,
        out_specs=(P(("cache", "tp"), None), P("cache", "tp", None, None)),
        check_vma=False,
    )
```

```python
import functools

import jax
import jax.numpy as jnp
from jax import lax
from jax.experimental import pallas as pl
from jax.experimental.pallas import tpu as pltpu
from jax.sharding import PartitionSpec as P

DK = 128
DV = 128
CH = 64
MAXCH = 2
R_DEV = 16
HEADS = 4
PAIRS = HEADS // 2
CACHE = 32
N_TP = 4
CK_DEV = 2
CHIP_SHIFTS = (2, 1, 3)
D = 2304
TILES = 3
PAIR = 2 * DK
ROWS = MAXCH * CH
TAG_ROWS = 16
READY = 4
GROUP = 4
VMEM_BYTES = 60 << 20
UNPACK_BYTES = 8 << 20
QUARTER_SHIFTS = (2, 1, 3, 0)

f32 = jnp.float32
bf16 = jnp.bfloat16


def chip_and_core(index):
    return index // 8, index // 2 % 4, index % 2


def chip_ordinal(shift):
    return jnp.where(shift == 1, 2, jnp.where(shift == 2, 1, shift))


def block_diagonal(left, right):
    zeros = jnp.zeros_like(left)
    return jnp.concatenate(
        [jnp.concatenate([left, zeros], axis=1), jnp.concatenate([zeros, right], axis=1)],
        axis=0,
    )


def pair_diagonal(pair):
    return block_diagonal(pair[:, :DK], pair[:, DK:])


def side_by_side(left, right):
    return jnp.concatenate([left, right], axis=1)


def prepare_kernel(
    pair,
    q_ref,
    k_ref,
    v_ref,
    g_ref,
    b_ref,
    m_ref,
    gate_ref,
    gain_ref,
    wq_ref,
    u_ref,
    lk_ref,
    d_ref,
    gain_out_ref,
    decay_ref,
):
    step = pl.program_id(0)
    lower = lax.broadcasted_iota(jnp.int32, (CH, CH), 0) >= lax.broadcasted_iota(
        jnp.int32, (CH, CH), 1
    )
    summing = jnp.where(lower, 1.0, 0.0).astype(bf16)
    row = lax.broadcasted_iota(jnp.int32, (CH, 2 * CH), 0)
    column = lax.broadcasted_iota(jnp.int32, (CH, 2 * CH), 1)
    causal = row >= lax.rem(column, CH)
    first_half = column[:1] < CH
    gain = gain_ref[...]
    decays = []
    for r in range(READY):
        strengths = [
            b_ref[2 * pair + side : 2 * pair + side + 1, pl.ds(r * ROWS, ROWS)]
            for side in range(2)
        ]
        turned = [pltpu.roll(strength, CH, 1) for strength in strengths]
        for c in range(MAXCH):
            rows = pl.ds(r * ROWS + c * CH, CH)
            cumulative = jnp.dot(summing, g_ref[rows, :], preferred_element_type=f32)
            query_fwd, key_fwd, key_back, key_end, plain_values = [], [], [], [], []
            for side in range(2):
                lanes = pl.ds(side * DK, DK)
                q = q_ref[rows, lanes].astype(f32)
                k = k_ref[rows, lanes].astype(f32)
                cum = cumulative[:, side * DK : (side + 1) * DK]
                last = cum[CH - 1 : CH, :]
                forward = jnp.exp(cum)
                q_scale = lax.rsqrt(jnp.sum(q * q, axis=1, keepdims=True) + 1e-06)
                k_unit = k * lax.rsqrt(jnp.sum(k * k, axis=1, keepdims=True) + 1e-06)
                query_fwd.append((q * q_scale * forward).astype(bf16))
                key_fwd.append((k_unit * forward).astype(bf16))
                key_back.append((k_unit * jnp.exp(-cum)).astype(bf16))
                key_end.append(k_unit * jnp.exp(last - cum))
                plain_values.append(v_ref[rows, lanes])
                decays.append(jnp.exp(last))
                gate = jax.nn.sigmoid(gate_ref[rows, lanes].astype(f32))
                gain_out_ref[rows, lanes] = (gain * gate).astype(bf16)
            if c == 0:
                strength = jnp.where(first_half, strengths[0], turned[1])
            else:
                strength = jnp.where(first_half, turned[0], strengths[1])
            inverse = (m_ref[r * MAXCH + c] * strength).astype(bf16)
            w = jnp.dot(inverse, block_diagonal(*key_fwd), preferred_element_type=f32)
            u = jnp.dot(inverse, block_diagonal(*plain_values), preferred_element_type=f32)
            queries = side_by_side(*query_fwd)
            scores = lax.dot_general(
                queries,
                block_diagonal(*key_back),
                (((1,), (1,)), ((), ())),
                preferred_element_type=f32,
            )
            wq_ref[r, c, pl.ds(0, CH), :] = w.astype(bf16)
            wq_ref[r, c, pl.ds(CH, CH), :] = queries
            u_ref[r, c] = u.astype(bf16)
            lk_ref[r, c, pl.ds(0, CH), :] = jnp.where(causal, scores, 0.0).astype(bf16)
            lk_ref[r, c, pl.ds(CH, DK), :] = jnp.concatenate(key_end, axis=0).T.astype(bf16)
    decay_ref[pl.ds(pl.multiple_of(step * READY * 4, 8), READY * 4), :] = jnp.concatenate(
        decays, axis=0
    )

    @pl.when(step == R_DEV // READY - 1)
    def _():
        d_ref[...] = decay_ref[...].T


def advance_kernel(
    owner_ref,
    slot_ref,
    ret_ref,
    counts_ref,
    *refs,
):
    sources, refs = refs[:-22], refs[-22:]
    ready, gated_outs, send_ref = refs[:5], refs[5:9], refs[9]
    wq_ref, u_ref, lk_ref, d_ref, gain_ref, initial_ref, gated_ref, final_ref = refs[10:18]
    ready_sems, in_sems, gated_sems, out_sems = refs[18:]

    here_x, here_y, here_core = chip_and_core(lax.axis_index("cache"))
    z = lax.axis_index("tp")
    order = [lax.rem(z + shift, N_TP) for shift in QUARTER_SHIFTS]

    def request_of(place):
        return order[place // GROUP] * GROUP + place % GROUP

    def whereabouts(place):
        owner, slot = owner_ref[request_of(place)], slot_ref[request_of(place)]
        if len(sources) == 1:
            return 0, owner * CK_DEV + slot
        chip_x, chip_y, core = chip_and_core(owner)
        away_x = chip_ordinal(lax.rem(here_x - chip_x + 4, 4))
        away_y = chip_ordinal(lax.rem(here_y - chip_y + 4, 4))
        first = jnp.where(core == 0, away_x, away_y)
        second = jnp.where(core == 0, away_y, away_x)
        return second + jnp.where(core == here_core, 0, 4), first * CK_DEV + slot

    def ready_copies(quarter):
        at = pl.ds(order[quarter] * GROUP, GROUP)
        tokens = pl.ds(order[quarter] * GROUP * ROWS, GROUP * ROWS)
        where = (at, at, at, tokens)
        sources = (ready[0], ready[1], ready[2], ready[4])
        return [
            pltpu.make_async_copy(
                source.at[where[n]], target.at[quarter], ready_sems.at[quarter * 4 + n]
            )
            for n, (source, target) in enumerate(zip(sources, (wq_ref, u_ref, lk_ref, gain_ref)))
        ]

    def decay_copy():
        return pltpu.make_async_copy(ready[3], d_ref, ready_sems.at[N_TP * 4])

    def copy_in(place, source, row):
        return pltpu.make_async_copy(
            source.at[row, pl.ds(0, PAIR)], initial_ref.at[place], in_sems.at[place]
        )

    def copy_out(place):
        return pltpu.make_async_copy(
            final_ref.at[place], send_ref.at[ret_ref[request_of(place)]], out_sems.at[place]
        )

    def start_states(quarter):
        for place in range(quarter * GROUP, (quarter + 1) * GROUP):
            chosen, row = whereabouts(place)
            for index, source in enumerate(sources):

                @pl.when(chosen == index)
                def _(place=place, source=source, row=row):
                    copy_in(place, source, row).start()

    def stretch(quarter, c, states, diagonals, decays):
        reads = [
            jnp.dot(wq_ref[quarter, r, c], diagonals[r], preferred_element_type=f32)
            for r in range(GROUP)
        ]
        news = [
            (u_ref[quarter, r, c].astype(f32) - reads[r][:CH]).astype(bf16) for r in range(GROUP)
        ]
        writes = [
            jnp.dot(lk_ref[quarter, r, c], pair_diagonal(news[r]), preferred_element_type=f32)
            for r in range(GROUP)
        ]
        after = []
        for r in range(GROUP):
            sides = []
            for side in range(2):
                at = r * 4 + 2 * c + side
                lanes = slice(side * DV, (side + 1) * DV)
                decay = decays[:, at : at + 1]
                sides.append(decay * states[r][side] + writes[r][CH:, lanes])
            after.append(sides)
        return [reads[r][CH:] + writes[r][:CH] for r in range(GROUP)], after

    def put_gated(quarter, c, outs, lives):
        for r in range(GROUP):
            for side in range(2):
                rows, lanes = pl.ds(r * ROWS + c * CH, CH), pl.ds(side * DV, DV)
                head_out = outs[r][:, side * DV : (side + 1) * DV]
                mean_square = jnp.mean(head_out * head_out, axis=1, keepdims=True)
                gated = head_out * lax.rsqrt(mean_square + 1e-05)
                gated = gated * gain_ref[quarter, rows, lanes].astype(f32)
                if c > 0:
                    gated = jnp.where(lives[r], gated, 0.0)
                gated_ref[quarter, rows, lanes] = gated.astype(bf16)

    decay_copy().start()
    for quarter in range(N_TP):
        for copy in ready_copies(quarter):
            copy.start()
        if quarter < 2:
            start_states(quarter)
    decay_copy().wait()

    for quarter in range(N_TP):
        places = [quarter * GROUP + r for r in range(GROUP)]
        lives = [counts_ref[request_of(place)] > 1 for place in places]
        for copy in ready_copies(quarter):
            copy.wait()
        for place in places:
            copy_in(place, sources[0], 0).wait()
        stored = [
            [initial_ref[place, pl.ds(side * DK, DK), :] for side in range(2)] for place in places
        ]
        states = [[side.astype(f32) for side in sides] for sides in stored]
        decays = pltpu.roll(d_ref[...], DK - order[quarter] * GROUP * 4, 1)
        outs, states = stretch(
            quarter, 0, states, [block_diagonal(*sides) for sides in stored], decays
        )
        put_gated(quarter, 0, outs, lives)
        diagonals = [block_diagonal(*[side.astype(bf16) for side in sides]) for sides in states]
        outs, after = stretch(quarter, 1, states, diagonals, decays)
        for r, place in enumerate(places):
            for side in range(2):
                final = jnp.where(lives[r], after[r][side], states[r][side])
                final_ref[place, pl.ds(side * DK, DK), :] = final.astype(bf16)
            copy_out(place).start()
        put_gated(quarter, 1, outs, lives)
        if quarter + 2 < N_TP:
            start_states(quarter + 2)
        pltpu.make_async_copy(
            gated_ref.at[quarter], gated_outs[quarter], gated_sems.at[quarter]
        ).start()

    for quarter in range(N_TP):
        pltpu.make_async_copy(
            gated_ref.at[quarter], gated_outs[quarter], gated_sems.at[quarter]
        ).wait()
    for place in range(R_DEV):
        copy_out(place).wait()


def pack_kernel(owner_ref, store_ref, earlier_ref, later_ref):
    lane = lax.broadcasted_iota(jnp.int32, (TAG_ROWS, DV), 1)
    tag = jnp.zeros((TAG_ROWS, DV), jnp.int32)
    for r in range(R_DEV):
        tag = jnp.where(lane == r, owner_ref[r], tag)
    tag = tag.astype(f32).astype(bf16)
    for row in range(CK_DEV):
        for side in range(2):
            earlier_ref[row, pl.ds(side * DK, DK), :] = store_ref[row, side].astype(bf16)
            later_ref[row, pl.ds(side * DK, DK), :] = store_ref[row, 2 + side].astype(bf16)
        later_ref[row, pl.ds(PAIR, TAG_ROWS), :] = tag


def locate_kernel(tag_ref, source_ref):
    self_owner = lax.axis_index("cache").astype(f32)
    source = jnp.zeros((1, DV), f32)
    for block in range(CACHE):
        named = tag_ref[block].astype(f32)[:1, :] == self_owner
        source = source + jnp.where(named, float(block), 0.0)
    source_ref[...] = source.astype(jnp.int32)


def project_kernel(*refs):
    gated, own_ref, mine_ref, sibling_ref = refs[:8], refs[8], refs[9], refs[10]
    far_mine_ref, far_sibling_ref, out_ref = refs[11:]
    core = lax.axis_index("cache") % 2
    rows = jnp.concatenate([ref[...] for ref in gated], axis=1)

    def put(below_ref, above_ref, far_refs):
        weights = []
        for p in range(PAIRS):
            at = pl.ds(p * PAIR, PAIR)
            weights += [far_refs[p][...], below_ref[at, :], above_ref[at, :], own_ref[at, :]]
        out_ref[...] = jnp.dot(
            rows, jnp.concatenate(weights, axis=0), preferred_element_type=f32
        ).astype(bf16)

    @pl.when(core == 0)
    def _():
        put(mine_ref, sibling_ref, (far_mine_ref, far_sibling_ref))

    @pl.when(core == 1)
    def _():
        put(sibling_ref, mine_ref, (far_sibling_ref, far_mine_ref))


def unpack_kernel(pair, source_ref, received_ref, *refs):
    out_ref, slots_ref, states_ref, in_sems, out_sems = refs[-5:]

    def copy_in(place):
        return pltpu.make_async_copy(
            received_ref.at[source_ref[place]], slots_ref.at[place], in_sems.at[place]
        )

    def copy_out(place):
        return pltpu.make_async_copy(
            states_ref.at[place],
            out_ref.at[place, pl.ds(pair * PAIR, PAIR)],
            out_sems.at[place],
        )

    for place in range(R_DEV):
        copy_in(place).start()
    for place in range(R_DEV):
        copy_in(place).wait()
        states_ref[place] = slots_ref[place].astype(f32)
        copy_out(place).start()
    for place in range(R_DEV):
        copy_out(place).wait()


def pack(owners, ckpt_store):
    whole = pl.BlockSpec(memory_space=pltpu.VMEM)
    return pl.pallas_call(
        pack_kernel,
        in_specs=[pl.BlockSpec(memory_space=pltpu.SMEM), whole],
        out_shape=[
            jax.ShapeDtypeStruct((CK_DEV, PAIR, DV), bf16),
            jax.ShapeDtypeStruct((CK_DEV, PAIR + TAG_ROWS, DV), bf16),
        ],
        compiler_params=pltpu.CompilerParams(vmem_limit_bytes=VMEM_BYTES),
        cost_estimate=pl.CostEstimate(flops=0, bytes_accessed=800_000, transcendentals=0),
        name="pack",
    )(owners, ckpt_store)


def locate(gathered):
    return pl.pallas_call(
        locate_kernel,
        grid=(1,),
        in_specs=[pl.BlockSpec((CACHE, TAG_ROWS, DV), lambda i: (0, PAIR // TAG_ROWS, 0))],
        out_specs=pl.BlockSpec((1, DV), lambda i: (0, 0)),
        out_shape=jax.ShapeDtypeStruct((1, DV), jnp.int32),
        compiler_params=pltpu.CompilerParams(vmem_limit_bytes=VMEM_BYTES),
        cost_estimate=pl.CostEstimate(flops=0, bytes_accessed=200_000, transcendentals=0),
        name="locate",
    )(gathered.reshape(CACHE, -1, DV)).reshape(DV)


def prepare(pair, queries, key_vecs, values, log_decay, write_strength, inverses, out_gate, gain):
    token_rows = pl.BlockSpec((READY * ROWS, PAIR), lambda i: (i, pair))
    return pl.pallas_call(
        functools.partial(prepare_kernel, pair),
        grid=(R_DEV // READY,),
        in_specs=[token_rows] * 4
        + [
            pl.BlockSpec((HEADS, READY * ROWS), lambda i: (0, i)),
            pl.BlockSpec((READY * MAXCH, CH, 2 * CH), lambda i: (i, 0, pair)),
            token_rows,
            pl.BlockSpec((1, DV), lambda i: (0, 0)),
        ],
        out_specs=[
            pl.BlockSpec((READY, MAXCH, 2 * CH, PAIR), lambda i: (i, 0, 0, 0)),
            pl.BlockSpec((READY, MAXCH, CH, PAIR), lambda i: (i, 0, 0, 0)),
            pl.BlockSpec((READY, MAXCH, CH + DK, 2 * CH), lambda i: (i, 0, 0, 0)),
            pl.BlockSpec((DK, DK), lambda i: (0, 0)),
            pl.BlockSpec((READY * ROWS, PAIR), lambda i: (i, 0)),
        ],
        out_shape=[
            jax.ShapeDtypeStruct((R_DEV, MAXCH, 2 * CH, PAIR), bf16),
            jax.ShapeDtypeStruct((R_DEV, MAXCH, CH, PAIR), bf16),
            jax.ShapeDtypeStruct((R_DEV, MAXCH, CH + DK, 2 * CH), bf16),
            jax.ShapeDtypeStruct((DK, DK), f32),
            jax.ShapeDtypeStruct((R_DEV * ROWS, PAIR), bf16),
        ],
        scratch_shapes=[pltpu.VMEM((DK, DK), f32)],
        compiler_params=pltpu.CompilerParams(vmem_limit_bytes=VMEM_BYTES),
        cost_estimate=pl.CostEstimate(
            flops=400_000_000, bytes_accessed=14_000_000, transcendentals=2_000_000
        ),
        name="prepare",
    )(queries, key_vecs, values, log_decay, write_strength.T, inverses, out_gate, gain)


def advance(hit_owner, hit_slot, ret_owner, counts, sources, ready):
    anywhere = pl.BlockSpec(memory_space=pl.ANY)
    return pl.pallas_call(
        advance_kernel,
        grid_spec=pltpu.PrefetchScalarGridSpec(
            num_scalar_prefetch=4,
            grid=(1,),
            in_specs=[anywhere] * (len(sources) + len(ready)),
            out_specs=[anywhere] * (N_TP + 1),
            scratch_shapes=[
                pltpu.VMEM((N_TP, GROUP, MAXCH, 2 * CH, PAIR), bf16),
                pltpu.VMEM((N_TP, GROUP, MAXCH, CH, PAIR), bf16),
                pltpu.VMEM((N_TP, GROUP, MAXCH, CH + DK, 2 * CH), bf16),
                pltpu.VMEM((DK, DK), f32),
                pltpu.VMEM((N_TP, GROUP * ROWS, PAIR), bf16),
                pltpu.VMEM((R_DEV, PAIR, DV), bf16),
                pltpu.VMEM((N_TP, GROUP * ROWS, PAIR), bf16),
                pltpu.VMEM((R_DEV, PAIR, DV), bf16),
                pltpu.SemaphoreType.DMA((N_TP * 4 + 1,)),
                pltpu.SemaphoreType.DMA((R_DEV,)),
                pltpu.SemaphoreType.DMA((N_TP,)),
                pltpu.SemaphoreType.DMA((R_DEV,)),
            ],
        ),
        out_shape=[jax.ShapeDtypeStruct((GROUP * ROWS, PAIR), bf16)] * N_TP
        + [jax.ShapeDtypeStruct((CACHE, PAIR, DV), bf16)],
        compiler_params=pltpu.CompilerParams(vmem_limit_bytes=VMEM_BYTES),
        cost_estimate=pl.CostEstimate(
            flops=500_000_000, bytes_accessed=10_000_000, transcendentals=100_000
        ),
        name="advance",
    )(hit_owner, hit_slot, ret_owner, counts, *sources, *ready)


def project(gated, own_weight, weights):
    tile = D // TILES
    rows = gated[0].shape[0]
    weights = [own_weight, *weights]
    return pl.pallas_call(
        project_kernel,
        grid=(TILES,),
        in_specs=[pl.BlockSpec((rows, PAIR), lambda t: (0, 0))] * (PAIRS * N_TP)
        + [pl.BlockSpec((weight.shape[0], tile), lambda t: (0, t)) for weight in weights],
        out_specs=pl.BlockSpec((rows, tile), lambda t: (0, t)),
        out_shape=jax.ShapeDtypeStruct((rows, D), bf16),
        compiler_params=pltpu.CompilerParams(vmem_limit_bytes=VMEM_BYTES),
        cost_estimate=pl.CostEstimate(
            flops=4_800_000_000, bytes_accessed=14_000_000, transcendentals=0
        ),
        name="project",
    )(*gated, *weights)


def unpack(pair, source, received, before=None):
    kept = [] if before is None else [before]
    return pl.pallas_call(
        functools.partial(unpack_kernel, pair),
        grid_spec=pltpu.PrefetchScalarGridSpec(
            num_scalar_prefetch=1,
            grid=(1,),
            in_specs=[pl.BlockSpec(memory_space=pl.ANY)] * (1 + len(kept)),
            out_specs=pl.BlockSpec(memory_space=pl.ANY),
            scratch_shapes=[
                pltpu.VMEM((R_DEV, PAIR, DV), bf16),
                pltpu.VMEM((R_DEV, PAIR, DV), f32),
                pltpu.SemaphoreType.DMA((R_DEV,)),
                pltpu.SemaphoreType.DMA((R_DEV,)),
            ],
        ),
        out_shape=jax.ShapeDtypeStruct((R_DEV, HEADS * DK, DV), f32),
        input_output_aliases={2: 0} if kept else {},
        compiler_params=pltpu.CompilerParams(vmem_limit_bytes=UNPACK_BYTES),
        cost_estimate=pl.CostEstimate(flops=0, bytes_accessed=3_200_000, transcendentals=0),
        name="unpack",
    )(source, received, *kept)


def along_tp(x, shift):
    return lax.ppermute(x, "tp", [(z, (z + shift) % N_TP) for z in range(N_TP)])


def by_cores_along_tp(x):
    pairs = []
    for index in range(CACHE):
        for z in range(N_TP):
            to = (z + (1 if index % 2 == 0 else N_TP - 1)) % N_TP
            pairs.append((index * N_TP + z, index * N_TP + to))
    return lax.ppermute(x, ("cache", "tp"), pairs)


def to_sibling(x):
    return lax.ppermute(x, "cache", [(i, i ^ 1) for i in range(CACHE)])


def along_chips(x, turned, shift):
    pairs = []
    for index in range(CACHE):
        chip_x, chip_y, core = chip_and_core(index)
        if (core == 0) != turned:
            chip_x = (chip_x + shift) % 4
        else:
            chip_y = (chip_y + shift) % 4
        pairs.append((index, (chip_x * 4 + chip_y) * 2 + core))
    return lax.ppermute(x, "cache", pairs)


def gather_by_chips(mine, beside, work):
    line = jnp.concatenate(
        [mine] + [along_chips(mine, False, shift) for shift in CHIP_SHIFTS], axis=0
    )
    line, tokens = lax.optimization_barrier((line, beside[0]))
    beside = (tokens, beside[1])
    plane = [along_chips(line, True, shift) for shift in CHIP_SHIFTS]
    plane, done = lax.optimization_barrier((plane, work(beside)))
    plane = [line, *plane]
    return plane + [to_sibling(part) for part in plane], done


def body(
    queries,
    key_vecs,
    values,
    log_decay,
    write_strength,
    inverses,
    suffix_stretches,
    ckpt_store,
    hit_owner,
    hit_slot,
    ret_owner,
    out_gate,
    norm_gain,
    out_weight,
):
    earlier, later = pack(ret_owner, ckpt_store)
    later = lax.all_gather(later, "cache", axis=0, tiled=True)

    earlier, weight = lax.optimization_barrier((earlier, out_weight))
    near_weight = by_cores_along_tp(weight)
    shifts = QUARTER_SHIFTS[:3]

    tokens = (
        queries,
        key_vecs,
        values,
        log_decay,
        write_strength,
        inverses,
        out_gate,
        norm_gain.reshape(1, DV),
    )
    earlier, (ready, near_weight) = gather_by_chips(
        earlier, (tokens, near_weight), lambda beside: (prepare(0, *beside[0]), beside[1])
    )
    core = lax.rem(lax.axis_index("cache"), 2)
    far_weight = by_cores_along_tp(
        lax.dynamic_slice(near_weight, (core * PAIR, 0), (PAIR, D))
    )

    *gated, sending = advance(
        hit_owner, hit_slot, ret_owner, suffix_stretches, earlier, ready
    )
    received = [lax.all_to_all(sending, "cache", split_axis=0, concat_axis=0, tiled=True)]
    others = [along_tp(rows, shift) for rows, shift in zip(gated[:3], shifts)]
    gated_parts = others + [gated[3]]

    tokens, _ = lax.optimization_barrier((tokens, sending))
    ready = prepare(1, *tokens)
    *gated, sending = advance(
        hit_owner, hit_slot, ret_owner, suffix_stretches, [later], ready
    )
    sending, far_weight, _ = lax.optimization_barrier((sending, far_weight, others[1:]))
    received.append(lax.all_to_all(sending, "cache", split_axis=0, concat_axis=0, tiled=True))
    gated_parts += [along_tp(rows, shift) for rows, shift in zip(gated[:3], shifts)] + [gated[3]]

    weights = [near_weight, to_sibling(near_weight), far_weight, to_sibling(far_weight)]
    mixed = project(gated_parts, out_weight, weights)

    source = locate(later)
    new_ckpts = None
    for p in range(PAIRS):
        new_ckpts = unpack(p, source, received[p], new_ckpts)
    new_ckpts = new_ckpts.reshape(R_DEV, HEADS, DK, DV)
    return (mixed, new_ckpts)


def solution(mesh):
    placed = (
        P("cache", "tp"),
        P("cache", "tp"),
        P("cache", "tp"),
        P("cache", "tp"),
        P("cache", "tp"),
        P("cache", None, "tp"),
        P("cache"),
        P("cache", "tp", None, None),
        P("cache"),
        P("cache"),
        P("cache"),
        P("cache", "tp"),
        P(),
        P("tp", None),
    )
    return jax.shard_map(
        body,
        mesh=mesh,
        in_specs=placed,
        out_specs=(P(("cache", "tp"), None), P("cache", "tp", None, None)),
        check_vma=False,
    )
```

```python
import functools

import jax
import jax.numpy as jnp
from jax import lax
from jax.experimental import pallas as pl
from jax.experimental.pallas import tpu as pltpu
from jax.sharding import PartitionSpec as P

DK = 128
DV = 128
CH = 64
MAXCH = 2
R_DEV = 16
HEADS = 4
PAIRS = HEADS // 2
CACHE = 32
N_TP = 4
CK_DEV = 2
CHIP_SHIFTS = (2, 1, 3)
D = 2304
TILES = 3
PAIR = 2 * DK
ROWS = MAXCH * CH
TAG_ROWS = 16
READY = 4
GROUP = 4
VMEM_BYTES = 60 << 20
PROJECT_BYTES = 32 << 20
UNPACK_BYTES = 8 << 20
QUARTER_SHIFTS = (2, 1, 3, 0)

f32 = jnp.float32
bf16 = jnp.bfloat16


def chip_and_core(index):
    return index // 8, index // 2 % 4, index % 2


def chip_ordinal(shift):
    return jnp.where(shift == 1, 2, jnp.where(shift == 2, 1, shift))


def block_diagonal(left, right):
    zeros = jnp.zeros_like(left)
    return jnp.concatenate(
        [jnp.concatenate([left, zeros], axis=1), jnp.concatenate([zeros, right], axis=1)],
        axis=0,
    )


def pair_diagonal(pair):
    return block_diagonal(pair[:, :DK], pair[:, DK:])


def side_by_side(left, right):
    return jnp.concatenate([left, right], axis=1)


def prepare_kernel(
    pair,
    q_ref,
    k_ref,
    v_ref,
    g_ref,
    b_ref,
    m_ref,
    gate_ref,
    gain_ref,
    wq_ref,
    u_ref,
    lk_ref,
    d_ref,
    gain_out_ref,
    decay_ref,
):
    step = pl.program_id(0)
    lower = lax.broadcasted_iota(jnp.int32, (CH, CH), 0) >= lax.broadcasted_iota(
        jnp.int32, (CH, CH), 1
    )
    summing = jnp.where(lower, 1.0, 0.0).astype(bf16)
    row = lax.broadcasted_iota(jnp.int32, (CH, 2 * CH), 0)
    column = lax.broadcasted_iota(jnp.int32, (CH, 2 * CH), 1)
    causal = row >= lax.rem(column, CH)
    first_half = column[:1] < CH
    gain = gain_ref[...]
    decays = []
    for r in range(READY):
        strengths = [
            b_ref[2 * pair + side : 2 * pair + side + 1, pl.ds(r * ROWS, ROWS)]
            for side in range(2)
        ]
        turned = [pltpu.roll(strength, CH, 1) for strength in strengths]
        for c in range(MAXCH):
            rows = pl.ds(r * ROWS + c * CH, CH)
            cumulative = jnp.dot(summing, g_ref[rows, :], preferred_element_type=f32)
            query_fwd, key_fwd, key_back, key_end, plain_values = [], [], [], [], []
            for side in range(2):
                lanes = pl.ds(side * DK, DK)
                q = q_ref[rows, lanes].astype(f32)
                k = k_ref[rows, lanes].astype(f32)
                cum = cumulative[:, side * DK : (side + 1) * DK]
                last = cum[CH - 1 : CH, :]
                forward = jnp.exp(cum)
                q_scale = lax.rsqrt(jnp.sum(q * q, axis=1, keepdims=True) + 1e-06)
                k_unit = k * lax.rsqrt(jnp.sum(k * k, axis=1, keepdims=True) + 1e-06)
                query_fwd.append((q * q_scale * forward).astype(bf16))
                key_fwd.append((k_unit * forward).astype(bf16))
                key_back.append((k_unit * jnp.exp(-cum)).astype(bf16))
                key_end.append(k_unit * jnp.exp(last - cum))
                plain_values.append(v_ref[rows, lanes])
                decays.append(jnp.exp(last))
                gate = jax.nn.sigmoid(gate_ref[rows, lanes].astype(f32))
                gain_out_ref[rows, lanes] = (gain * gate).astype(bf16)
            if c == 0:
                strength = jnp.where(first_half, strengths[0], turned[1])
            else:
                strength = jnp.where(first_half, turned[0], strengths[1])
            inverse = (m_ref[r * MAXCH + c] * strength).astype(bf16)
            w = jnp.dot(inverse, block_diagonal(*key_fwd), preferred_element_type=f32)
            u = jnp.dot(inverse, block_diagonal(*plain_values), preferred_element_type=f32)
            queries = side_by_side(*query_fwd)
            scores = lax.dot_general(
                queries,
                block_diagonal(*key_back),
                (((1,), (1,)), ((), ())),
                preferred_element_type=f32,
            )
            wq_ref[r, c, pl.ds(0, CH), :] = w.astype(bf16)
            wq_ref[r, c, pl.ds(CH, CH), :] = queries
            u_ref[r, c] = u.astype(bf16)
            lk_ref[r, c, pl.ds(0, CH), :] = jnp.where(causal, scores, 0.0).astype(bf16)
            lk_ref[r, c, pl.ds(CH, DK), :] = jnp.concatenate(key_end, axis=0).T.astype(bf16)
    decay_ref[pl.ds(pl.multiple_of(step * READY * 4, 8), READY * 4), :] = jnp.concatenate(
        decays, axis=0
    )

    @pl.when(step == R_DEV // READY - 1)
    def _():
        d_ref[...] = decay_ref[...].T


def advance_kernel(
    owner_ref,
    slot_ref,
    ret_ref,
    counts_ref,
    *refs,
):
    sources, refs = refs[:-22], refs[-22:]
    ready, gated_outs, send_ref = refs[:5], refs[5:9], refs[9]
    wq_ref, u_ref, lk_ref, d_ref, gain_ref, initial_ref, gated_ref, final_ref = refs[10:18]
    ready_sems, in_sems, gated_sems, out_sems = refs[18:]

    here_x, here_y, here_core = chip_and_core(lax.axis_index("cache"))
    z = lax.axis_index("tp")
    order = [lax.rem(z + shift, N_TP) for shift in QUARTER_SHIFTS]

    def request_of(place):
        return order[place // GROUP] * GROUP + place % GROUP

    def whereabouts(place):
        owner, slot = owner_ref[request_of(place)], slot_ref[request_of(place)]
        if len(sources) == 1:
            return 0, owner * CK_DEV + slot
        chip_x, chip_y, core = chip_and_core(owner)
        away_x = chip_ordinal(lax.rem(here_x - chip_x + 4, 4))
        away_y = chip_ordinal(lax.rem(here_y - chip_y + 4, 4))
        first = jnp.where(core == 0, away_x, away_y)
        second = jnp.where(core == 0, away_y, away_x)
        return second + jnp.where(core == here_core, 0, 4), first * CK_DEV + slot

    def ready_copies(quarter):
        at = pl.ds(order[quarter] * GROUP, GROUP)
        tokens = pl.ds(order[quarter] * GROUP * ROWS, GROUP * ROWS)
        where = (at, at, at, tokens)
        sources = (ready[0], ready[1], ready[2], ready[4])
        return [
            pltpu.make_async_copy(
                source.at[where[n]], target.at[quarter], ready_sems.at[quarter * 4 + n]
            )
            for n, (source, target) in enumerate(zip(sources, (wq_ref, u_ref, lk_ref, gain_ref)))
        ]

    def decay_copy():
        return pltpu.make_async_copy(ready[3], d_ref, ready_sems.at[N_TP * 4])

    def copy_in(place, source, row):
        return pltpu.make_async_copy(
            source.at[row, pl.ds(0, PAIR)], initial_ref.at[place], in_sems.at[place]
        )

    def copy_out(place):
        return pltpu.make_async_copy(
            final_ref.at[place], send_ref.at[ret_ref[request_of(place)]], out_sems.at[place]
        )

    def start_states(quarter):
        for place in range(quarter * GROUP, (quarter + 1) * GROUP):
            chosen, row = whereabouts(place)
            for index, source in enumerate(sources):

                @pl.when(chosen == index)
                def _(place=place, source=source, row=row):
                    copy_in(place, source, row).start()

    def stretch(quarter, c, states, diagonals, decays):
        reads = [
            jnp.dot(wq_ref[quarter, r, c], diagonals[r], preferred_element_type=f32)
            for r in range(GROUP)
        ]
        news = [
            (u_ref[quarter, r, c].astype(f32) - reads[r][:CH]).astype(bf16) for r in range(GROUP)
        ]
        writes = [
            jnp.dot(lk_ref[quarter, r, c], pair_diagonal(news[r]), preferred_element_type=f32)
            for r in range(GROUP)
        ]
        after = []
        for r in range(GROUP):
            sides = []
            for side in range(2):
                at = r * 4 + 2 * c + side
                lanes = slice(side * DV, (side + 1) * DV)
                decay = decays[:, at : at + 1]
                sides.append(decay * states[r][side] + writes[r][CH:, lanes])
            after.append(sides)
        return [reads[r][CH:] + writes[r][:CH] for r in range(GROUP)], after

    def put_gated(quarter, c, outs, lives):
        for r in range(GROUP):
            for side in range(2):
                rows, lanes = pl.ds(r * ROWS + c * CH, CH), pl.ds(side * DV, DV)
                head_out = outs[r][:, side * DV : (side + 1) * DV]
                mean_square = jnp.mean(head_out * head_out, axis=1, keepdims=True)
                gated = head_out * lax.rsqrt(mean_square + 1e-05)
                gated = gated * gain_ref[quarter, rows, lanes].astype(f32)
                if c > 0:
                    gated = jnp.where(lives[r], gated, 0.0)
                gated_ref[quarter, rows, lanes] = gated.astype(bf16)

    decay_copy().start()
    for quarter in range(N_TP):
        for copy in ready_copies(quarter):
            copy.start()
        if quarter < 2:
            start_states(quarter)
    decay_copy().wait()

    for quarter in range(N_TP):
        places = [quarter * GROUP + r for r in range(GROUP)]
        lives = [counts_ref[request_of(place)] > 1 for place in places]
        for copy in ready_copies(quarter):
            copy.wait()
        for place in places:
            copy_in(place, sources[0], 0).wait()
        stored = [
            [initial_ref[place, pl.ds(side * DK, DK), :] for side in range(2)] for place in places
        ]
        states = [[side.astype(f32) for side in sides] for sides in stored]
        decays = pltpu.roll(d_ref[...], DK - order[quarter] * GROUP * 4, 1)
        outs, states = stretch(
            quarter, 0, states, [block_diagonal(*sides) for sides in stored], decays
        )
        put_gated(quarter, 0, outs, lives)
        diagonals = [block_diagonal(*[side.astype(bf16) for side in sides]) for sides in states]
        outs, after = stretch(quarter, 1, states, diagonals, decays)
        for r, place in enumerate(places):
            for side in range(2):
                final = jnp.where(lives[r], after[r][side], states[r][side])
                final_ref[place, pl.ds(side * DK, DK), :] = final.astype(bf16)
            copy_out(place).start()
        put_gated(quarter, 1, outs, lives)
        if quarter + 2 < N_TP:
            start_states(quarter + 2)
        pltpu.make_async_copy(
            gated_ref.at[quarter], gated_outs[quarter], gated_sems.at[quarter]
        ).start()

    for quarter in range(N_TP):
        pltpu.make_async_copy(
            gated_ref.at[quarter], gated_outs[quarter], gated_sems.at[quarter]
        ).wait()
    for place in range(R_DEV):
        copy_out(place).wait()


def pack_kernel(owner_ref, store_ref, earlier_ref, later_ref):
    lane = lax.broadcasted_iota(jnp.int32, (TAG_ROWS, DV), 1)
    tag = jnp.zeros((TAG_ROWS, DV), jnp.int32)
    for r in range(R_DEV):
        tag = jnp.where(lane == r, owner_ref[r], tag)
    tag = tag.astype(f32).astype(bf16)
    for row in range(CK_DEV):
        for side in range(2):
            earlier_ref[row, pl.ds(side * DK, DK), :] = store_ref[row, side].astype(bf16)
            later_ref[row, pl.ds(side * DK, DK), :] = store_ref[row, 2 + side].astype(bf16)
        later_ref[row, pl.ds(PAIR, TAG_ROWS), :] = tag


def locate_kernel(tag_ref, source_ref):
    self_owner = lax.axis_index("cache").astype(f32)
    source = jnp.zeros((1, DV), f32)
    for block in range(CACHE):
        named = tag_ref[block].astype(f32)[:1, :] == self_owner
        source = source + jnp.where(named, float(block), 0.0)
    source_ref[...] = source.astype(jnp.int32)


def project_kernel(*refs):
    gated, own_ref, mine_ref, sibling_ref = refs[:8], refs[8], refs[9], refs[10]
    far_mine_ref, far_sibling_ref, out_ref = refs[11:]
    core = lax.axis_index("cache") % 2
    rows = jnp.concatenate([ref[...] for ref in gated], axis=1)

    def put(below_ref, above_ref, far_refs):
        weights = []
        for p in range(PAIRS):
            at = pl.ds(p * PAIR, PAIR)
            weights += [far_refs[p][...], below_ref[at, :], above_ref[at, :], own_ref[at, :]]
        out_ref[...] = jnp.dot(
            rows, jnp.concatenate(weights, axis=0), preferred_element_type=f32
        ).astype(bf16)

    @pl.when(core == 0)
    def _():
        put(mine_ref, sibling_ref, (far_mine_ref, far_sibling_ref))

    @pl.when(core == 1)
    def _():
        put(sibling_ref, mine_ref, (far_sibling_ref, far_mine_ref))


def unpack_kernel(pair, source_ref, received_ref, *refs):
    out_ref, slots_ref, states_ref, in_sems, out_sems = refs[-5:]

    def copy_in(place):
        return pltpu.make_async_copy(
            received_ref.at[source_ref[place]], slots_ref.at[place], in_sems.at[place]
        )

    def copy_out(place):
        return pltpu.make_async_copy(
            states_ref.at[place],
            out_ref.at[place, pl.ds(pair * PAIR, PAIR)],
            out_sems.at[place],
        )

    for place in range(R_DEV):
        copy_in(place).start()
    for place in range(R_DEV):
        copy_in(place).wait()
        states_ref[place] = slots_ref[place].astype(f32)
        copy_out(place).start()
    for place in range(R_DEV):
        copy_out(place).wait()


def pack(owners, ckpt_store):
    whole = pl.BlockSpec(memory_space=pltpu.VMEM)
    return pl.pallas_call(
        pack_kernel,
        in_specs=[pl.BlockSpec(memory_space=pltpu.SMEM), whole],
        out_shape=[
            jax.ShapeDtypeStruct((CK_DEV, PAIR, DV), bf16),
            jax.ShapeDtypeStruct((CK_DEV, PAIR + TAG_ROWS, DV), bf16),
        ],
        compiler_params=pltpu.CompilerParams(vmem_limit_bytes=VMEM_BYTES),
        cost_estimate=pl.CostEstimate(flops=0, bytes_accessed=800_000, transcendentals=0),
        name="pack",
    )(owners, ckpt_store)


def locate(gathered):
    return pl.pallas_call(
        locate_kernel,
        grid=(1,),
        in_specs=[pl.BlockSpec((CACHE, TAG_ROWS, DV), lambda i: (0, PAIR // TAG_ROWS, 0))],
        out_specs=pl.BlockSpec((1, DV), lambda i: (0, 0)),
        out_shape=jax.ShapeDtypeStruct((1, DV), jnp.int32),
        compiler_params=pltpu.CompilerParams(vmem_limit_bytes=VMEM_BYTES),
        cost_estimate=pl.CostEstimate(flops=0, bytes_accessed=200_000, transcendentals=0),
        name="locate",
    )(gathered.reshape(CACHE, -1, DV)).reshape(DV)


def prepare(pair, queries, key_vecs, values, log_decay, write_strength, inverses, out_gate, gain):
    token_rows = pl.BlockSpec((READY * ROWS, PAIR), lambda i: (i, pair))
    return pl.pallas_call(
        functools.partial(prepare_kernel, pair),
        grid=(R_DEV // READY,),
        in_specs=[token_rows] * 4
        + [
            pl.BlockSpec((HEADS, READY * ROWS), lambda i: (0, i)),
            pl.BlockSpec((READY * MAXCH, CH, 2 * CH), lambda i: (i, 0, pair)),
            token_rows,
            pl.BlockSpec((1, DV), lambda i: (0, 0)),
        ],
        out_specs=[
            pl.BlockSpec((READY, MAXCH, 2 * CH, PAIR), lambda i: (i, 0, 0, 0)),
            pl.BlockSpec((READY, MAXCH, CH, PAIR), lambda i: (i, 0, 0, 0)),
            pl.BlockSpec((READY, MAXCH, CH + DK, 2 * CH), lambda i: (i, 0, 0, 0)),
            pl.BlockSpec((DK, DK), lambda i: (0, 0)),
            pl.BlockSpec((READY * ROWS, PAIR), lambda i: (i, 0)),
        ],
        out_shape=[
            jax.ShapeDtypeStruct((R_DEV, MAXCH, 2 * CH, PAIR), bf16),
            jax.ShapeDtypeStruct((R_DEV, MAXCH, CH, PAIR), bf16),
            jax.ShapeDtypeStruct((R_DEV, MAXCH, CH + DK, 2 * CH), bf16),
            jax.ShapeDtypeStruct((DK, DK), f32),
            jax.ShapeDtypeStruct((R_DEV * ROWS, PAIR), bf16),
        ],
        scratch_shapes=[pltpu.VMEM((DK, DK), f32)],
        compiler_params=pltpu.CompilerParams(vmem_limit_bytes=VMEM_BYTES),
        cost_estimate=pl.CostEstimate(
            flops=400_000_000, bytes_accessed=14_000_000, transcendentals=2_000_000
        ),
        name="prepare",
    )(queries, key_vecs, values, log_decay, write_strength.T, inverses, out_gate, gain)


def advance(hit_owner, hit_slot, ret_owner, counts, sources, ready):
    anywhere = pl.BlockSpec(memory_space=pl.ANY)
    return pl.pallas_call(
        advance_kernel,
        grid_spec=pltpu.PrefetchScalarGridSpec(
            num_scalar_prefetch=4,
            grid=(1,),
            in_specs=[anywhere] * (len(sources) + len(ready)),
            out_specs=[anywhere] * (N_TP + 1),
            scratch_shapes=[
                pltpu.VMEM((N_TP, GROUP, MAXCH, 2 * CH, PAIR), bf16),
                pltpu.VMEM((N_TP, GROUP, MAXCH, CH, PAIR), bf16),
                pltpu.VMEM((N_TP, GROUP, MAXCH, CH + DK, 2 * CH), bf16),
                pltpu.VMEM((DK, DK), f32),
                pltpu.VMEM((N_TP, GROUP * ROWS, PAIR), bf16),
                pltpu.VMEM((R_DEV, PAIR, DV), bf16),
                pltpu.VMEM((N_TP, GROUP * ROWS, PAIR), bf16),
                pltpu.VMEM((R_DEV, PAIR, DV), bf16),
                pltpu.SemaphoreType.DMA((N_TP * 4 + 1,)),
                pltpu.SemaphoreType.DMA((R_DEV,)),
                pltpu.SemaphoreType.DMA((N_TP,)),
                pltpu.SemaphoreType.DMA((R_DEV,)),
            ],
        ),
        out_shape=[jax.ShapeDtypeStruct((GROUP * ROWS, PAIR), bf16)] * N_TP
        + [jax.ShapeDtypeStruct((CACHE, PAIR, DV), bf16)],
        compiler_params=pltpu.CompilerParams(vmem_limit_bytes=VMEM_BYTES),
        cost_estimate=pl.CostEstimate(
            flops=500_000_000, bytes_accessed=10_000_000, transcendentals=100_000
        ),
        name="advance",
    )(hit_owner, hit_slot, ret_owner, counts, *sources, *ready)


def project(gated, own_weight, weights):
    tile = D // TILES
    rows = gated[0].shape[0]
    weights = [own_weight, *weights]
    return pl.pallas_call(
        project_kernel,
        grid=(TILES,),
        in_specs=[pl.BlockSpec((rows, PAIR), lambda t: (0, 0))] * (PAIRS * N_TP)
        + [pl.BlockSpec((weight.shape[0], tile), lambda t: (0, t)) for weight in weights],
        out_specs=pl.BlockSpec((rows, tile), lambda t: (0, t)),
        out_shape=jax.ShapeDtypeStruct((rows, D), bf16),
        compiler_params=pltpu.CompilerParams(vmem_limit_bytes=PROJECT_BYTES),
        cost_estimate=pl.CostEstimate(
            flops=4_800_000_000, bytes_accessed=14_000_000, transcendentals=0
        ),
        name="project",
    )(*gated, *weights)


def unpack(pair, source, received, before=None):
    kept = [] if before is None else [before]
    return pl.pallas_call(
        functools.partial(unpack_kernel, pair),
        grid_spec=pltpu.PrefetchScalarGridSpec(
            num_scalar_prefetch=1,
            grid=(1,),
            in_specs=[pl.BlockSpec(memory_space=pl.ANY)] * (1 + len(kept)),
            out_specs=pl.BlockSpec(memory_space=pl.ANY),
            scratch_shapes=[
                pltpu.VMEM((R_DEV, PAIR, DV), bf16),
                pltpu.VMEM((R_DEV, PAIR, DV), f32),
                pltpu.SemaphoreType.DMA((R_DEV,)),
                pltpu.SemaphoreType.DMA((R_DEV,)),
            ],
        ),
        out_shape=jax.ShapeDtypeStruct((R_DEV, HEADS * DK, DV), f32),
        input_output_aliases={2: 0} if kept else {},
        compiler_params=pltpu.CompilerParams(vmem_limit_bytes=UNPACK_BYTES),
        cost_estimate=pl.CostEstimate(flops=0, bytes_accessed=3_200_000, transcendentals=0),
        name="unpack",
    )(source, received, *kept)


def along_tp(x, shift):
    return lax.ppermute(x, "tp", [(z, (z + shift) % N_TP) for z in range(N_TP)])


def by_cores_along_tp(x):
    pairs = []
    for index in range(CACHE):
        for z in range(N_TP):
            to = (z + (1 if index % 2 == 0 else N_TP - 1)) % N_TP
            pairs.append((index * N_TP + z, index * N_TP + to))
    return lax.ppermute(x, ("cache", "tp"), pairs)


def to_sibling(x):
    return lax.ppermute(x, "cache", [(i, i ^ 1) for i in range(CACHE)])


def along_chips(x, turned, shift):
    pairs = []
    for index in range(CACHE):
        chip_x, chip_y, core = chip_and_core(index)
        if (core == 0) != turned:
            chip_x = (chip_x + shift) % 4
        else:
            chip_y = (chip_y + shift) % 4
        pairs.append((index, (chip_x * 4 + chip_y) * 2 + core))
    return lax.ppermute(x, "cache", pairs)


def gather_by_chips(mine, beside, work):
    line = jnp.concatenate(
        [mine] + [along_chips(mine, False, shift) for shift in CHIP_SHIFTS], axis=0
    )
    line, tokens = lax.optimization_barrier((line, beside[0]))
    beside = (tokens, beside[1])
    plane = [along_chips(line, True, shift) for shift in CHIP_SHIFTS]
    plane, done = lax.optimization_barrier((plane, work(beside)))
    plane = [line, *plane]
    return plane + [to_sibling(part) for part in plane], done


def body(
    queries,
    key_vecs,
    values,
    log_decay,
    write_strength,
    inverses,
    suffix_stretches,
    ckpt_store,
    hit_owner,
    hit_slot,
    ret_owner,
    out_gate,
    norm_gain,
    out_weight,
):
    earlier, later = pack(ret_owner, ckpt_store)
    later = lax.all_gather(later, "cache", axis=0, tiled=True)

    earlier, weight = lax.optimization_barrier((earlier, out_weight))
    near_weight = by_cores_along_tp(weight)
    shifts = QUARTER_SHIFTS[:3]

    tokens = (
        queries,
        key_vecs,
        values,
        log_decay,
        write_strength,
        inverses,
        out_gate,
        norm_gain.reshape(1, DV),
    )
    earlier, (ready, near_weight) = gather_by_chips(
        earlier, (tokens, near_weight), lambda beside: (prepare(0, *beside[0]), beside[1])
    )
    core = lax.rem(lax.axis_index("cache"), 2)
    far_weight = by_cores_along_tp(
        lax.dynamic_slice(near_weight, (core * PAIR, 0), (PAIR, D))
    )

    *gated, sending = advance(
        hit_owner, hit_slot, ret_owner, suffix_stretches, earlier, ready
    )
    received = [lax.all_to_all(sending, "cache", split_axis=0, concat_axis=0, tiled=True)]
    others = [along_tp(rows, shift) for rows, shift in zip(gated[:3], shifts)]
    gated_parts = others + [gated[3]]

    tokens, _ = lax.optimization_barrier((tokens, sending))
    ready = prepare(1, *tokens)
    *gated, sending = advance(
        hit_owner, hit_slot, ret_owner, suffix_stretches, [later], ready
    )
    sending, far_weight, _ = lax.optimization_barrier((sending, far_weight, others[1:]))
    received.append(lax.all_to_all(sending, "cache", split_axis=0, concat_axis=0, tiled=True))
    gated_parts += [along_tp(rows, shift) for rows, shift in zip(gated[:3], shifts)] + [gated[3]]

    weights = [near_weight, to_sibling(near_weight), far_weight, to_sibling(far_weight)]
    mixed = project(gated_parts, out_weight, weights)

    source = locate(later)
    new_ckpts = None
    for p in range(PAIRS):
        new_ckpts = unpack(p, source, received[p], new_ckpts)
    new_ckpts = new_ckpts.reshape(R_DEV, HEADS, DK, DV)
    return (mixed, new_ckpts)


def solution(mesh):
    placed = (
        P("cache", "tp"),
        P("cache", "tp"),
        P("cache", "tp"),
        P("cache", "tp"),
        P("cache", "tp"),
        P("cache", None, "tp"),
        P("cache"),
        P("cache", "tp", None, None),
        P("cache"),
        P("cache"),
        P("cache"),
        P("cache", "tp"),
        P(),
        P("tp", None),
    )
    return jax.shard_map(
        body,
        mesh=mesh,
        in_specs=placed,
        out_specs=(P(("cache", "tp"), None), P("cache", "tp", None, None)),
        check_vma=False,
    )
```
